32 devices in a mesh: group: 2 (over x), seq: 8 (over z, y), head: 2 (over core).
Axes of the slice: x: 2, y: 2, z: 4, core: 2. Of those that a mesh axis runs over, the one named last changes fastest.
Arguments:
- queries: bfloat16 [4096, 4096], P(('group', 'seq'), 'head'), parts along dimension 0, may hold values from -600 to 600
- image_token_rows: bfloat16 [6656, 8192], P(('group', 'seq')), parts along dimension 0, may hold values from -6 to 6
- key_matrix: bfloat16 [8192, 512], P('seq', 'head'), may hold values from -0.0625 to 0.0625
- value_matrix: bfloat16 [8192, 512], P('seq', 'head'), may hold values from -0.0625 to 0.0625
- k_gain: float32 [128], replicated, may hold values from 0.5 to 1.5
- image_counts: int32 [4], P('group'), parts along dimension 0, may hold values from 800 to 1601, as said below
- image_lo: int32 [4096], P(('group', 'seq')), parts along dimension 0, may hold values from 0 to 1, as said below
- image_hi: int32 [4096], P(('group', 'seq')), parts along dimension 0, may hold values from 1 to 2
- gate: float32 [1], replicated, may hold values from 0.3 to 1.2
Outputs:
- attended: bfloat16 [4096, 4096], P(('group', 'seq'), 'head'), parts along dimension 0
The draws below stay inside these ranges and needn't reach their ends.
There are 2 independent parts, one for each index of `group`. The reference program is written for one: setup_inputs(seed, part) draws one part's arguments, and reference() takes and returns one part's arrays. A program takes and returns all parts, laid end to end along the dimension named above; an argument that names none is the same for every part. Nothing has to cross between parts.
Inputs may be any that keep to these rules, and one draw needn't show every extreme that they name: `image_counts`: each image has at least 800 tokens (half, rounded down); some image has exactly 1601. image_lo[t] < image_hi[t] for every text token.
All inputs are finite; a program needn't handle non-finite values.
Results may differ from the reference program's by a relative error of at most 0.012.
The reference program's roundings to bfloat16 on the way (of `values`, `key_rows` and `rounded_weights`) count: a program that leaves them out, or rounds other values in their place, can miss the bound.
Values may be sent and summed in bfloat16 or wider, within the bound.
No kernel may reach another device: no remote copies, remote signals or barrier semaphores. Data moves between devices by JAX's collectives and lax.ppermute only.
A program may use at most 192 MiB of HBM per device.

```python
import math
import jax
import jax.numpy as jnp
from jax import lax

MODEL_WIDTH = 8192
HQ = 32
KEY_VALUE_HEADS = 4
HEAD_SIZE = 128
QUERY_GROUP = 8
IMG_TOK = 1601
SLOT = 1664
NIMG = 2
IMAGE_SLOTS = 3328
TEXT_TOKENS = 2048


def image_pair(key):
    first = jax.random.randint(jax.random.fold_in(key, 101), (TEXT_TOKENS,), 0, NIMG)
    second = jax.random.randint(jax.random.fold_in(key, 102), (TEXT_TOKENS,), 0, NIMG)
    return (jnp.minimum(first, second).astype(jnp.int32), (jnp.maximum(first, second) + 1).astype(jnp.int32))


def draw_image_lo(key, part):
    lower, upper = image_pair(key)
    return lower


def draw_image_hi(key, part):
    lower, upper = image_pair(key)
    return upper


def draw_image_counts(key, part):
    key = jax.random.fold_in(key, 5)
    base_counts = jax.random.randint(jax.random.fold_in(key, 1), (NIMG,), IMG_TOK // 2, IMG_TOK + 1)
    chosen = jax.random.randint(jax.random.fold_in(key, 2), (), 0, NIMG)
    return jnp.where(jnp.arange(NIMG) == chosen, IMG_TOK, base_counts).astype(jnp.int32)


def draw_queries(key, part):
    key = jax.random.fold_in(key, 7)
    sample = 2.0 * jax.random.normal(jax.random.fold_in(key, 3), (TEXT_TOKENS, HQ * HEAD_SIZE), jnp.float32)
    return jnp.clip(sample, -600.0, 600.0).astype(jnp.bfloat16)


def block_levels(stream_key, extent, cuts, smallest, top_value):
    factor_of, own = 1.0, jax.random.fold_in(stream_key, 6)
    for axis_at, shards_of in cuts:
        steps = jnp.exp(jax.random.uniform(jax.random.fold_in(own, axis_at), (shards_of,), jnp.float32, smallest / len(cuts), top_value / len(cuts)))
        factor_of = factor_of * jnp.repeat(steps, extent[axis_at] // shards_of).reshape([-1 if axis == axis_at else 1 for axis in range(len(extent))])
    return factor_of


def gaussian(key, shape, width, reach, shards=(), dtype=jnp.bfloat16):
    values = jax.random.normal(key, shape, jnp.float32) * width
    if len(shards) > 0:
        values = block_levels(key, shape, shards, -0.22, 0.18) * values
    return jnp.clip(values, min=-reach, max=reach).astype(dtype)


def setup_inputs(seed: int = 0, part: int = 0) -> dict:
    key_list = jax.random.split(jax.random.key(seed), 10)
    own_keys = jax.random.split(jax.random.fold_in(key_list[9], part), 10)
    queries = draw_queries(jax.random.fold_in(jax.random.fold_in(key_list[9], part), 71), part)
    image_token_rows = gaussian(own_keys[1], (IMAGE_SLOTS, MODEL_WIDTH), 1.0, 6.0, ((0, 8),))
    key_matrix = gaussian(key_list[2], (MODEL_WIDTH, KEY_VALUE_HEADS * HEAD_SIZE), MODEL_WIDTH ** -0.5, 0.0625, ((0, 8), (1, 2)))
    value_matrix = gaussian(key_list[3], (MODEL_WIDTH, KEY_VALUE_HEADS * HEAD_SIZE), MODEL_WIDTH ** -0.5, 0.0625, ((0, 8), (1, 2)))
    k_gain = jnp.clip(jax.random.uniform(key_list[4], (HEAD_SIZE,), jnp.float32, 0.5, 1.5), 0.5, 1.5)
    image_counts = draw_image_counts(jax.random.fold_in(jax.random.fold_in(key_list[9], part), 71), part)
    image_lo = draw_image_lo(jax.random.fold_in(jax.random.fold_in(key_list[9], part), 71), part)
    image_hi = draw_image_hi(jax.random.fold_in(jax.random.fold_in(key_list[9], part), 71), part)
    gate = jnp.clip(jax.random.uniform(key_list[8], (1,), jnp.float32, 0.3, 1.2), 0.3, 1.2)
    return {"queries": queries, "image_token_rows": image_token_rows, "key_matrix": key_matrix, "value_matrix": value_matrix, "k_gain": k_gain, "image_counts": image_counts, "image_lo": image_lo, "image_hi": image_hi, "gate": gate}


def reference(queries, image_token_rows, key_matrix, value_matrix, k_gain, image_counts, image_lo, image_hi, gate):
    key_projected = jnp.dot(image_token_rows, key_matrix, preferred_element_type=jnp.float32).reshape(IMAGE_SLOTS, KEY_VALUE_HEADS, HEAD_SIZE)
    value_rows = jnp.dot(image_token_rows, value_matrix, preferred_element_type=jnp.float32).astype(jnp.bfloat16).reshape(IMAGE_SLOTS, KEY_VALUE_HEADS, HEAD_SIZE)
    inverse = lax.rsqrt(lax.optimization_barrier(jnp.mean(key_projected * key_projected, axis=-1, keepdims=True)) + 1e-05)
    key_rows = (key_projected * inverse * k_gain).astype(jnp.bfloat16)
    position = jnp.arange(IMAGE_SLOTS)
    picture = position // SLOT
    in_image = position - picture * SLOT < image_counts[picture]
    text_token_block = math.gcd(TEXT_TOKENS, 512)
    grouped_queries = queries.reshape(TEXT_TOKENS // text_token_block, text_token_block, KEY_VALUE_HEADS, QUERY_GROUP, HEAD_SIZE)
    low_rows = image_lo.reshape(TEXT_TOKENS // text_token_block, text_token_block)
    high_rows = image_hi.reshape(TEXT_TOKENS // text_token_block, text_token_block)
    keys_wide = key_rows.astype(jnp.float32)
    values_wide = value_rows.astype(jnp.float32)

    def attend(pieces):
        query_block, low_block, high_block = pieces
        scores = jnp.einsum('tgqd,pgd->tgqp', query_block.astype(jnp.float32), keys_wide) / math.sqrt(HEAD_SIZE)
        allowed = in_image[None, :] & (low_block[:, None] <= picture[None, :]) & (picture[None, :] < high_block[:, None])
        allowed = allowed[:, None, None, :]
        masked = jnp.where(allowed, scores, -1e+30)
        highest = lax.optimization_barrier(jnp.max(masked, axis=-1, keepdims=True))
        weights_raw = jnp.where(allowed, jnp.exp(masked - highest), 0.0)
        denominator = lax.optimization_barrier(jnp.sum(weights_raw, axis=-1, keepdims=True))
        rounded_weights = weights_raw.astype(jnp.bfloat16)
        numerator = jnp.einsum('tgqp,pgd->tgqd', rounded_weights.astype(jnp.float32), values_wide)
        gated = jnp.tanh(gate[0]) * (numerator / denominator)
        return gated.reshape(text_token_block, HQ * HEAD_SIZE).astype(jnp.bfloat16)
    return lax.map(attend, (grouped_queries, low_rows, high_rows)).reshape(TEXT_TOKENS, HQ * HEAD_SIZE)
```

```python
import functools
import math

import jax
import jax.numpy as jnp
from jax import lax
from jax.experimental import pallas as pl
from jax.experimental.pallas import tpu as pltpu
from jax.sharding import PartitionSpec as P

HEAD_SIZE = 128
QUERY_GROUP = 8
SLOT = 1664
NIMG = 2
CHUNK = 256
BIG = 2.0**98


def attention_kernel(info, q_ref, flag_ref, gate_ref, kv_ref, o_ref, keys, vals, scores):
    rows = kv_ref.shape[0]
    piece_rows = info[NIMG]

    @pl.when(pl.program_id(0) == 0)
    def _():
        lane = lax.broadcasted_iota(jnp.int32, (CHUNK, HEAD_SIZE), 1)
        row = lax.broadcasted_iota(jnp.int32, (CHUNK, HEAD_SIZE), 0)
        ones = jnp.where(lane == 0, 1.0, 0.0).astype(jnp.bfloat16)
        for start in range(0, rows, CHUNK):
            at = slice(start, start + CHUNK)
            position = row + start
            flags = jnp.zeros((CHUNK, HEAD_SIZE), jnp.float32)
            for i in range(NIMG):
                mine = (position >= i * SLOT) & (position < (i + 1) * SLOT)
                beyond = mine & (position - i * SLOT >= info[i])
                hit = (mine & (lane == i)) | (beyond & (lane == NIMG))
                flags = jnp.where(hit, -BIG, flags)
            keys[at, :HEAD_SIZE] = kv_ref[at, :HEAD_SIZE]
            keys[at, HEAD_SIZE:] = flags.astype(jnp.bfloat16)
            vals[at, :HEAD_SIZE] = kv_ref[at, HEAD_SIZE:]
            vals[at, HEAD_SIZE:] = ones

    scale = math.log2(math.e) / math.sqrt(HEAD_SIZE)
    wide = jnp.concatenate([q_ref[...], flag_ref[...]], axis=1)
    highest = None
    for start in range(0, rows, CHUNK):
        part = lax.dot_general(
            wide,
            keys[start : start + CHUNK, :],
            (((1,), (1,)), ((), ())),
            preferred_element_type=jnp.float32,
        )
        scores[:, start : start + CHUNK] = part
        best = jnp.maximum(part[:, :HEAD_SIZE], part[:, HEAD_SIZE:])
        highest = best if highest is None else jnp.maximum(highest, best)
    top = jnp.max(highest, axis=1, keepdims=True)
    weights = jnp.exp2((scores[...] - top) * scale).astype(jnp.bfloat16)
    total = jnp.dot(weights, vals[...], preferred_element_type=jnp.float32)
    gain = jnp.tanh(gate_ref[...])
    out = gain * (total[:, :HEAD_SIZE] / total[:, HEAD_SIZE : HEAD_SIZE + 1])
    o_ref[...] = out.astype(o_ref.dtype)


def attend(queries, flags, gate_row, kv, info, head, previous):
    text_rows, width = queries.shape
    rows = kv.shape[0]
    grid_spec = pltpu.PrefetchScalarGridSpec(
        num_scalar_prefetch=1,
        grid=(QUERY_GROUP,),
        in_specs=[
            pl.BlockSpec((text_rows, HEAD_SIZE), lambda g, s: (0, head * QUERY_GROUP + g)),
            pl.BlockSpec((text_rows, HEAD_SIZE), lambda g, s: (0, 0)),
            pl.BlockSpec((1, HEAD_SIZE), lambda g, s: (0, 0)),
            pl.BlockSpec((rows, 2 * HEAD_SIZE), lambda g, s: (0, 0)),
        ]
        + ([] if previous is None else [pl.BlockSpec(memory_space=pl.ANY)]),
        out_specs=pl.BlockSpec((text_rows, HEAD_SIZE), lambda g, s: (0, head * QUERY_GROUP + g)),
        scratch_shapes=[
            pltpu.VMEM((rows, 2 * HEAD_SIZE), jnp.bfloat16),
            pltpu.VMEM((rows, 2 * HEAD_SIZE), jnp.bfloat16),
            pltpu.VMEM((text_rows, rows), jnp.float32),
        ],
    )

    def kernel(info_ref, q_ref, flag_ref, gate_ref, kv_ref, *rest):
        attention_kernel(info_ref, q_ref, flag_ref, gate_ref, kv_ref, *rest[-4:])

    args = (info, queries, flags, gate_row, kv)
    aliases = {}
    if previous is not None:
        args = args + (previous,)
        aliases = {5: 0}
    return pl.pallas_call(
        kernel,
        out_shape=jax.ShapeDtypeStruct((text_rows, width), jnp.bfloat16),
        grid_spec=grid_spec,
        input_output_aliases=aliases,
        compiler_params=pltpu.CompilerParams(vmem_limit_bytes=40 * 2**20),
        cost_estimate=pl.CostEstimate(
            flops=8 * QUERY_GROUP * text_rows * rows * HEAD_SIZE,
            bytes_accessed=2 * rows * 2 * HEAD_SIZE,
            transcendentals=QUERY_GROUP * text_rows * rows,
        ),
    )(*args)


def text_flags(image_lo, image_hi):
    lane = jnp.arange(HEAD_SIZE)[None, :]
    hidden = (lane < NIMG) & ((lane < image_lo[:, None]) | (lane >= image_hi[:, None]))
    return (hidden | (lane == NIMG)).astype(jnp.bfloat16)


def per_device(
    queries,
    image_token_rows,
    key_matrix,
    value_matrix,
    k_gain,
    image_counts,
    image_lo,
    image_hi,
    gate,
):
    img_rows = image_token_rows.shape[0]
    local_width = key_matrix.shape[1]
    local_heads = local_width // HEAD_SIZE
    key_projected = jnp.dot(
        image_token_rows,
        lax.all_gather(key_matrix, "seq", axis=0, tiled=True),
        preferred_element_type=jnp.float32,
    )
    value_proj = jnp.dot(
        image_token_rows,
        lax.all_gather(value_matrix, "seq", axis=0, tiled=True),
        preferred_element_type=jnp.float32,
    )
    flags = text_flags(image_lo, image_hi)
    gate_row = jnp.broadcast_to(gate[:, None], (1, HEAD_SIZE))
    info = jnp.concatenate([image_counts, jnp.full((1,), img_rows, jnp.int32)])
    out = None
    for head in range(local_heads):
        at = slice(head * HEAD_SIZE, (head + 1) * HEAD_SIZE)
        key_head = key_projected[:, at]
        inverse = lax.rsqrt(jnp.mean(key_head * key_head, axis=-1, keepdims=True) + 1e-05)
        key_head = (key_head * inverse * k_gain).astype(jnp.bfloat16)
        both = jnp.concatenate([key_head, value_proj[:, at].astype(jnp.bfloat16)], axis=1)
        kv = lax.all_gather(both, "seq", axis=0, tiled=True)
        out = attend(queries, flags, gate_row, kv, info, head, out)
    return out


def solution(mesh):
    in_specs = (
        P(("group", "seq"), "head"),
        P(("group", "seq"), None),
        P("seq", "head"),
        P("seq", "head"),
        P(),
        P("group"),
        P(("group", "seq")),
        P(("group", "seq")),
        P(),
    )
    out_specs = P(("group", "seq"), "head")
    return jax.shard_map(
        per_device, mesh=mesh, in_specs=in_specs, out_specs=out_specs, check_vma=False
    )
```

```python
import functools
import math

import jax
import jax.numpy as jnp
from jax import lax
from jax.experimental import pallas as pl
from jax.experimental.pallas import tpu as pltpu
from jax.sharding import PartitionSpec as P

HEAD_SIZE = 128
QUERY_GROUP = 8
SLOT = 1664
NIMG = 2
CHUNK = 256
BIG = 2.0**98


def attention_kernel(slots, info, q_ref, flag_ref, gate_ref, *refs):
    kv_refs = refs[:slots]
    o_ref, keys, vals, scores = refs[-4:]
    piece = kv_refs[0].shape[0]
    rows = slots * piece

    @pl.when(pl.program_id(0) == 0)
    def _():
        lane = lax.broadcasted_iota(jnp.int32, (piece, HEAD_SIZE), 1)
        row = lax.broadcasted_iota(jnp.int32, (piece, HEAD_SIZE), 0)
        ones = jnp.where(lane == 0, 1.0, 0.0).astype(jnp.bfloat16)
        for j, kv_ref in enumerate(kv_refs):
            at = slice(j * piece, (j + 1) * piece)
            position = row + info[NIMG + j] * piece
            flags = jnp.zeros((piece, HEAD_SIZE), jnp.float32)
            for i in range(NIMG):
                mine = (position >= i * SLOT) & (position < (i + 1) * SLOT)
                beyond = mine & (position - i * SLOT >= info[i])
                hit = (mine & (lane == i)) | (beyond & (lane == NIMG))
                flags = jnp.where(hit, -BIG, flags)
            keys[at, :HEAD_SIZE] = kv_ref[:, :HEAD_SIZE]
            keys[at, HEAD_SIZE:] = flags.astype(jnp.bfloat16)
            vals[at, :HEAD_SIZE] = kv_ref[:, HEAD_SIZE:]
            vals[at, HEAD_SIZE:] = ones

    scale = math.log2(math.e) / math.sqrt(HEAD_SIZE)
    wide = jnp.concatenate([q_ref[...], flag_ref[...]], axis=1)
    highest = None
    for start in range(0, rows, CHUNK):
        part = lax.dot_general(
            wide,
            keys[start : start + CHUNK, :],
            (((1,), (1,)), ((), ())),
            preferred_element_type=jnp.float32,
        )
        scores[:, start : start + CHUNK] = part
        best = jnp.maximum(part[:, :HEAD_SIZE], part[:, HEAD_SIZE:])
        highest = best if highest is None else jnp.maximum(highest, best)
    top = jnp.max(highest, axis=1, keepdims=True)
    weights = jnp.exp2((scores[...] - top) * scale).astype(jnp.bfloat16)
    total = jnp.dot(weights, vals[...], preferred_element_type=jnp.float32)
    gain = jnp.tanh(gate_ref[...])
    out = gain * (total[:, :HEAD_SIZE] / total[:, HEAD_SIZE : HEAD_SIZE + 1])
    o_ref[...] = out.astype(o_ref.dtype)


def attend(queries, flags, gate_row, pieces, info, head, previous):
    text_rows, width = queries.shape
    slots = len(pieces)
    piece = pieces[0].shape[0]
    rows = slots * piece
    grid_spec = pltpu.PrefetchScalarGridSpec(
        num_scalar_prefetch=1,
        grid=(QUERY_GROUP,),
        in_specs=[
            pl.BlockSpec((text_rows, HEAD_SIZE), lambda g, s: (0, head * QUERY_GROUP + g)),
            pl.BlockSpec((text_rows, HEAD_SIZE), lambda g, s: (0, 0)),
            pl.BlockSpec((1, HEAD_SIZE), lambda g, s: (0, 0)),
        ]
        + [pl.BlockSpec((piece, 2 * HEAD_SIZE), lambda g, s: (0, 0))] * slots
        + ([] if previous is None else [pl.BlockSpec(memory_space=pl.ANY)]),
        out_specs=pl.BlockSpec((text_rows, HEAD_SIZE), lambda g, s: (0, head * QUERY_GROUP + g)),
        scratch_shapes=[
            pltpu.VMEM((rows, 2 * HEAD_SIZE), jnp.bfloat16),
            pltpu.VMEM((rows, 2 * HEAD_SIZE), jnp.bfloat16),
            pltpu.VMEM((text_rows, rows), jnp.float32),
        ],
    )
    args = (info, queries, flags, gate_row, *pieces)
    aliases = {}
    if previous is not None:
        aliases = {len(args): 0}
        args = args + (previous,)
    return pl.pallas_call(
        functools.partial(attention_kernel, slots),
        out_shape=jax.ShapeDtypeStruct((text_rows, width), jnp.bfloat16),
        grid_spec=grid_spec,
        input_output_aliases=aliases,
        compiler_params=pltpu.CompilerParams(vmem_limit_bytes=40 * 2**20),
        cost_estimate=pl.CostEstimate(
            flops=8 * QUERY_GROUP * text_rows * rows * HEAD_SIZE,
            bytes_accessed=2 * rows * 2 * HEAD_SIZE,
            transcendentals=QUERY_GROUP * text_rows * rows,
        ),
    )(*args)


def text_flags(image_lo, image_hi):
    lane = jnp.arange(HEAD_SIZE)[None, :]
    hidden = (lane < NIMG) & ((lane < image_lo[:, None]) | (lane >= image_hi[:, None]))
    return (hidden | (lane == NIMG)).astype(jnp.bfloat16)


def pick_blocks(which, image, width):
    rows = image.shape[0]
    count = which.shape[0]

    def kernel(which_ref, image_ref, o_ref):
        o_ref[0] = image_ref[...]

    return pl.pallas_call(
        kernel,
        out_shape=jax.ShapeDtypeStruct((count, rows, width), image.dtype),
        grid_spec=pltpu.PrefetchScalarGridSpec(
            num_scalar_prefetch=1,
            grid=(count,),
            in_specs=[pl.BlockSpec((rows, width), lambda j, which: (0, which[j]))],
            out_specs=pl.BlockSpec((1, rows, width), lambda j, which: (j, 0, 0)),
        ),
        cost_estimate=pl.CostEstimate(
            flops=0, bytes_accessed=4 * count * rows * width, transcendentals=0
        ),
    )(which, image)


def project_own(which, image, weights, width):
    rows = image.shape[0]
    count = len(weights)
    columns = weights[0].shape[1]
    half = rows // 2

    def kernel(which_ref, *refs):
        total = None
        for j in range(count):
            term = jnp.dot(
                refs[j][...], refs[count + j][...], preferred_element_type=jnp.float32
            )
            total = term if total is None else total + term
        refs[-1][...] = total

    def block_of(j):
        return pl.BlockSpec((half, width), lambda i, which: (i, which[j]))

    return pl.pallas_call(
        kernel,
        out_shape=jax.ShapeDtypeStruct((rows, columns), jnp.float32),
        grid_spec=pltpu.PrefetchScalarGridSpec(
            num_scalar_prefetch=1,
            grid=(2,),
            in_specs=[block_of(j) for j in range(count)]
            + [pl.BlockSpec((width, columns), lambda i, which: (0, 0))] * count,
            out_specs=pl.BlockSpec((half, columns), lambda i, which: (i, 0)),
        ),
        compiler_params=pltpu.CompilerParams(vmem_limit_bytes=32 * 2**20),
        cost_estimate=pl.CostEstimate(
            flops=2 * count * rows * width * columns,
            bytes_accessed=2 * count * width * (rows + columns),
            transcendentals=0,
        ),
    )(which, *([image] * count), *weights)


def project_other(core, direct, passed, weights):
    each, rows, width = direct[0].shape
    chunks = len(direct)
    count = len(weights)
    columns = weights[0].shape[1]
    half = rows // 2

    def kernel(core_ref, *refs):
        direct_refs = refs[:chunks]
        passed_refs = refs[chunks : 2 * chunks]
        weight_refs = refs[2 * chunks : 2 * chunks + count]

        def run(first, second):
            total = None
            for start, group in ((0, first), (count // 2, second)):
                for a in range(chunks):
                    for i in range(each):
                        term = jnp.dot(
                            group[a][i],
                            weight_refs[start + a * each + i][...],
                            preferred_element_type=jnp.float32,
                        )
                        total = term if total is None else total + term
            refs[-1][...] = total

        @pl.when(core_ref[0] == 0)
        def _():
            run(direct_refs, passed_refs)

        @pl.when(core_ref[0] != 0)
        def _():
            run(passed_refs, direct_refs)

    return pl.pallas_call(
        kernel,
        out_shape=jax.ShapeDtypeStruct((rows, columns), jnp.float32),
        grid_spec=pltpu.PrefetchScalarGridSpec(
            num_scalar_prefetch=1,
            grid=(2,),
            in_specs=[pl.BlockSpec((each, half, width), lambda i, core: (0, i, 0))] * (2 * chunks)
            + [pl.BlockSpec((width, columns), lambda i, core: (0, 0))] * count,
            out_specs=pl.BlockSpec((half, columns), lambda i, core: (i, 0)),
        ),
        compiler_params=pltpu.CompilerParams(vmem_limit_bytes=32 * 2**20),
        cost_estimate=pl.CostEstimate(
            flops=2 * count * rows * width * columns,
            bytes_accessed=2 * count * width * (rows + columns),
            transcendentals=0,
        ),
    )(core, *direct, *passed, *weights)


def spread(own, far, near):
    def ring(step):
        return [
            (f * near + n, ((f + step) % far) * near + n) for f in range(far) for n in range(near)
        ]

    swap = [(i, i ^ 1) for i in range(far * near)]
    around = [own] + [None] * (far - 1)
    around[1] = lax.ppermute(own, "seq", ring(1))
    around[far - 1] = lax.ppermute(own, "seq", ring(far - 1))
    for k in range(2, far - 1):
        around[k] = lax.ppermute(around[k - 1], "seq", ring(1))
    pieces = []
    for piece in around:
        pieces += [piece, lax.ppermute(piece, "seq", swap)]
    return pieces


def finish(total, k_gain):
    key_head = total[:, :HEAD_SIZE]
    inverse = lax.rsqrt(jnp.mean(key_head * key_head, axis=-1, keepdims=True) + 1e-05)
    key_head = (key_head * inverse * k_gain).astype(jnp.bfloat16)
    return jnp.concatenate([key_head, total[:, HEAD_SIZE:].astype(jnp.bfloat16)], axis=1)


def per_device(
    seq_size,
    queries,
    image_token_rows,
    key_matrix,
    value_matrix,
    k_gain,
    image_counts,
    image_lo,
    image_hi,
    gate,
):
    img_rows, model_width = image_token_rows.shape
    local_heads = key_matrix.shape[1] // HEAD_SIZE
    flags = text_flags(image_lo, image_hi)
    gate_row = jnp.broadcast_to(gate[:, None], (1, HEAD_SIZE))
    group = lax.axis_index("group")
    core = lax.axis_index("head")
    index = lax.axis_index("seq")

    def head_weights(head):
        at = slice(head * HEAD_SIZE, (head + 1) * HEAD_SIZE)
        return jnp.concatenate([key_matrix[:, at], value_matrix[:, at]], axis=1)

    out = None
    if seq_size != 8 or img_rows % 32 or lax.axis_size("group") != 2:
        info = jnp.concatenate([image_counts, jnp.zeros((1,), jnp.int32)])
        for head in range(local_heads):
            weights = lax.all_gather(head_weights(head), "seq", axis=0, tiled=True)
            total = jnp.dot(image_token_rows, weights, preferred_element_type=jnp.float32)
            kv = lax.all_gather(finish(total, k_gain), "seq", axis=0, tiled=True)
            out = attend(queries, flags, gate_row, [kv], info, head, out)
        return out

    near = 2
    far = seq_size // near
    mine_far, mine_near = index // near, index % near
    shards = jnp.stack(
        [((mine_far - k) % far) * near + (mine_near ^ b) for k in range(far) for b in range(near)]
    ).astype(jnp.int32)
    info = jnp.concatenate([image_counts, shards])
    width = model_width // seq_size // 2
    across = [(0, 1), (1, 0)]
    chunks = 2
    each = seq_size // 2 // chunks
    direct, passed = [], []
    for a in range(chunks):
        slots = lax.dynamic_slice_in_dim(shards, core * (seq_size // 2) + a * each, each)
        block = pick_blocks(2 * slots + (1 - group), image_token_rows, width)
        direct.append(lax.ppermute(block, "group", across))
    passed = [lax.ppermute(block, "head", across) for block in direct]
    own_blocks = 2 * shards + group
    core_arg = core.reshape(1).astype(jnp.int32)
    heads_kv = []
    for head in range(local_heads):
        part = lax.dynamic_slice_in_dim(head_weights(head), group * width, width)
        weights = spread(part, far, near)
        own = project_own(own_blocks, image_token_rows, weights, width)
        other = project_other(core_arg, direct, passed, weights)
        total = own + lax.ppermute(other, "group", across)
        heads_kv.append(spread(finish(total, k_gain), far, near))
    for head in range(local_heads):
        out = attend(queries, flags, gate_row, heads_kv[head], info, head, out)
    return out


def solution(mesh):
    in_specs = (
        P(("group", "seq"), "head"),
        P(("group", "seq"), None),
        P("seq", "head"),
        P("seq", "head"),
        P(),
        P("group"),
        P(("group", "seq")),
        P(("group", "seq")),
        P(),
    )
    out_specs = P(("group", "seq"), "head")
    return jax.shard_map(
        functools.partial(per_device, mesh.shape["seq"]),
        mesh=mesh,
        in_specs=in_specs,
        out_specs=out_specs,
        check_vma=False,
    )
```

```python
import functools
import math

import jax
import jax.numpy as jnp
from jax import lax
from jax.experimental import pallas as pl
from jax.experimental.pallas import tpu as pltpu
from jax.sharding import PartitionSpec as P

HEAD_SIZE = 128
QUERY_GROUP = 8
SLOT = 1664
NIMG = 2
CHUNK = 256
HEADS_AT_ONCE = 4
ORDER = True
BIG = 2.0**98


def attention_kernel(slots, info, q_ref, flag_ref, gate_ref, *refs):
    kv_refs = refs[:slots]
    o_ref, keys, vals, *buffers = refs[-5:]
    piece = kv_refs[0].shape[0]
    rows = slots * piece

    @pl.when(pl.program_id(0) == 0)
    def _():
        lane = lax.broadcasted_iota(jnp.int32, (piece, HEAD_SIZE), 1)
        row = lax.broadcasted_iota(jnp.int32, (piece, HEAD_SIZE), 0)
        ones = jnp.where(lane == 0, 1.0, 0.0).astype(jnp.bfloat16)
        for j, kv_ref in enumerate(kv_refs):
            at = slice(j * piece, (j + 1) * piece)
            position = row + info[NIMG + j] * piece
            flags = jnp.zeros((piece, HEAD_SIZE), jnp.float32)
            for i in range(NIMG):
                mine = (position >= i * SLOT) & (position < (i + 1) * SLOT)
                beyond = mine & (position - i * SLOT >= info[i])
                hit = (mine & (lane == i)) | (beyond & (lane == NIMG))
                flags = jnp.where(hit, -BIG, flags)
            keys[at, :HEAD_SIZE] = kv_ref[:, :HEAD_SIZE]
            keys[at, HEAD_SIZE:] = flags.astype(jnp.bfloat16)
            vals[at, :HEAD_SIZE] = kv_ref[:, HEAD_SIZE:]
            vals[at, HEAD_SIZE:] = ones

    scale = math.log2(math.e) / math.sqrt(HEAD_SIZE)
    gain = jnp.tanh(gate_ref[...])
    top = None
    for i in range(HEADS_AT_ONCE + 1):
        now, later = buffers[(i + 1) % 2], buffers[i % 2]
        highest = total = None
        if i < HEADS_AT_ONCE:
            at = slice(i * HEAD_SIZE, (i + 1) * HEAD_SIZE)
            wide = jnp.concatenate([q_ref[:, at], flag_ref[...]], axis=1)
        for start in range(0, rows, CHUNK):
            chunk = slice(start, start + CHUNK)
            if i < HEADS_AT_ONCE:
                part = lax.dot_general(
                    wide,
                    keys[chunk, :],
                    (((1,), (1,)), ((), ())),
                    preferred_element_type=jnp.float32,
                )
                later[:, chunk] = part
                best = jnp.maximum(part[:, :HEAD_SIZE], part[:, HEAD_SIZE:])
                highest = best if highest is None else jnp.maximum(highest, best)
            if i > 0:
                weights = jnp.exp2((now[:, chunk] - top) * scale).astype(jnp.bfloat16)
                term = jnp.dot(weights, vals[chunk, :], preferred_element_type=jnp.float32)
                total = term if total is None else total + term
        if i > 0:
            at = slice((i - 1) * HEAD_SIZE, i * HEAD_SIZE)
            out = gain * (total[:, :HEAD_SIZE] / total[:, HEAD_SIZE : HEAD_SIZE + 1])
            o_ref[:, at] = out.astype(o_ref.dtype)
        if i < HEADS_AT_ONCE:
            top = jnp.max(highest, axis=1, keepdims=True)


def attend(queries, flags, gate_row, pieces, info, head, previous):
    text_rows, width = queries.shape
    slots = len(pieces)
    piece = pieces[0].shape[0]
    rows = slots * piece
    steps = QUERY_GROUP // HEADS_AT_ONCE
    block = HEADS_AT_ONCE * HEAD_SIZE
    grid_spec = pltpu.PrefetchScalarGridSpec(
        num_scalar_prefetch=1,
        grid=(steps,),
        in_specs=[
            pl.BlockSpec((text_rows, block), lambda g, s: (0, head * steps + g)),
            pl.BlockSpec((text_rows, HEAD_SIZE), lambda g, s: (0, 0)),
            pl.BlockSpec((1, HEAD_SIZE), lambda g, s: (0, 0)),
        ]
        + [pl.BlockSpec((piece, 2 * HEAD_SIZE), lambda g, s: (0, 0))] * slots
        + ([] if previous is None else [pl.BlockSpec(memory_space=pl.ANY)]),
        out_specs=pl.BlockSpec((text_rows, block), lambda g, s: (0, head * steps + g)),
        scratch_shapes=[
            pltpu.VMEM((rows, 2 * HEAD_SIZE), jnp.bfloat16),
            pltpu.VMEM((rows, 2 * HEAD_SIZE), jnp.bfloat16),
            pltpu.VMEM((text_rows, rows), jnp.float32),
            pltpu.VMEM((text_rows, rows), jnp.float32),
        ],
    )
    args = (info, queries, flags, gate_row, *pieces)
    aliases = {}
    if previous is not None:
        aliases = {len(args): 0}
        args = args + (previous,)
    return pl.pallas_call(
        functools.partial(attention_kernel, slots),
        out_shape=jax.ShapeDtypeStruct((text_rows, width), jnp.bfloat16),
        grid_spec=grid_spec,
        input_output_aliases=aliases,
        compiler_params=pltpu.CompilerParams(vmem_limit_bytes=40 * 2**20),
        cost_estimate=pl.CostEstimate(
            flops=8 * QUERY_GROUP * text_rows * rows * HEAD_SIZE,
            bytes_accessed=2 * rows * 2 * HEAD_SIZE,
            transcendentals=QUERY_GROUP * text_rows * rows,
        ),
    )(*args)


def text_flags(image_lo, image_hi):
    lane = jnp.arange(HEAD_SIZE)[None, :]
    hidden = (lane < NIMG) & ((lane < image_lo[:, None]) | (lane >= image_hi[:, None]))
    return (hidden | (lane == NIMG)).astype(jnp.bfloat16)


def pick_blocks(which, image, width):
    rows = image.shape[0]
    count = which.shape[0]

    def kernel(which_ref, image_ref, o_ref, sems):
        copies = []
        for j in range(count):
            column = pl.multiple_of(which_ref[j] * width, width)
            copies.append(
                pltpu.make_async_copy(image_ref.at[:, pl.ds(column, width)], o_ref.at[j], sems.at[j])
            )
        for copy in copies:
            copy.start()
        for copy in copies:
            copy.wait()

    return pl.pallas_call(
        kernel,
        out_shape=jax.ShapeDtypeStruct((count, rows, width), image.dtype),
        grid_spec=pltpu.PrefetchScalarGridSpec(
            num_scalar_prefetch=1,
            grid=(),
            in_specs=[pl.BlockSpec(memory_space=pl.ANY)],
            out_specs=pl.BlockSpec(memory_space=pltpu.VMEM),
            scratch_shapes=[pltpu.SemaphoreType.DMA((count,))],
        ),
        cost_estimate=pl.CostEstimate(
            flops=0, bytes_accessed=4 * count * rows * width, transcendentals=0
        ),
    )(which, image)


def project_own(which, image, weights, width):
    rows = image.shape[0]
    count = len(weights)
    columns = weights[0].shape[1]
    half = rows // 2

    def kernel(which_ref, *refs):
        total = None
        for j in range(count):
            term = jnp.dot(
                refs[j][...], refs[count + j][...], preferred_element_type=jnp.float32
            )
            total = term if total is None else total + term
        refs[-1][...] = total

    def block_of(j):
        return pl.BlockSpec((half, width), lambda i, which: (i, which[j]))

    return pl.pallas_call(
        kernel,
        out_shape=jax.ShapeDtypeStruct((rows, columns), jnp.float32),
        grid_spec=pltpu.PrefetchScalarGridSpec(
            num_scalar_prefetch=1,
            grid=(2,),
            in_specs=[block_of(j) for j in range(count)]
            + [pl.BlockSpec((width, columns), lambda i, which: (0, 0))] * count,
            out_specs=pl.BlockSpec((half, columns), lambda i, which: (i, 0)),
        ),
        compiler_params=pltpu.CompilerParams(vmem_limit_bytes=32 * 2**20),
        cost_estimate=pl.CostEstimate(
            flops=2 * count * rows * width * columns,
            bytes_accessed=2 * count * width * (rows + columns),
            transcendentals=0,
        ),
    )(which, *([image] * count), *weights)


def project_other(core, direct, passed, weights):
    each, rows, width = direct[0].shape
    chunks = len(direct)
    count = len(weights)
    columns = weights[0].shape[1]
    half = rows // 2

    def kernel(core_ref, *refs):
        direct_refs = refs[:chunks]
        passed_refs = refs[chunks : 2 * chunks]
        weight_refs = refs[2 * chunks : 2 * chunks + count]

        def run(first, second):
            total = None
            for start, group in ((0, first), (count // 2, second)):
                for a in range(chunks):
                    for i in range(each):
                        term = jnp.dot(
                            group[a][i],
                            weight_refs[start + a * each + i][...],
                            preferred_element_type=jnp.float32,
                        )
                        total = term if total is None else total + term
            refs[-1][...] = total

        @pl.when(core_ref[0] == 0)
        def _():
            run(direct_refs, passed_refs)

        @pl.when(core_ref[0] != 0)
        def _():
            run(passed_refs, direct_refs)

    return pl.pallas_call(
        kernel,
        out_shape=jax.ShapeDtypeStruct((rows, columns), jnp.float32),
        grid_spec=pltpu.PrefetchScalarGridSpec(
            num_scalar_prefetch=1,
            grid=(2,),
            in_specs=[pl.BlockSpec((each, half, width), lambda i, core: (0, i, 0))] * (2 * chunks)
            + [pl.BlockSpec((width, columns), lambda i, core: (0, 0))] * count,
            out_specs=pl.BlockSpec((half, columns), lambda i, core: (i, 0)),
        ),
        compiler_params=pltpu.CompilerParams(vmem_limit_bytes=32 * 2**20),
        cost_estimate=pl.CostEstimate(
            flops=2 * count * rows * width * columns,
            bytes_accessed=2 * count * width * (rows + columns),
            transcendentals=0,
        ),
    )(core, *direct, *passed, *weights)


def after(value, *others):
    return lax.optimization_barrier((value, *others))[0]


def ring(far, near, step):
    return [(f * near + n, ((f + step) % far) * near + n) for f in range(far) for n in range(near)]


def swap(value, size):
    return lax.ppermute(value, "seq", [(i, i ^ 1) for i in range(size)])


def spread(own, far, near, hold=()):
    size = far * near
    begin = after(own, *hold)
    around = [own] + [None] * (far - 1)
    around[1] = lax.ppermute(begin, "seq", ring(far, near, 1))
    around[far - 1] = lax.ppermute(begin, "seq", ring(far, near, far - 1))
    for k in range(2, far - 1):
        around[k] = lax.ppermute(around[k - 1], "seq", ring(far, near, 1))
    pieces = []
    for piece in around:
        pieces += [piece, swap(piece, size)]
    return pieces


def finish(total, k_gain):
    key_head = total[:, :HEAD_SIZE]
    inverse = lax.rsqrt(jnp.mean(key_head * key_head, axis=-1, keepdims=True) + 1e-05)
    key_head = (key_head * inverse * k_gain).astype(jnp.bfloat16)
    return jnp.concatenate([key_head, total[:, HEAD_SIZE:].astype(jnp.bfloat16)], axis=1)


def per_device(
    seq_size,
    queries,
    image_token_rows,
    key_matrix,
    value_matrix,
    k_gain,
    image_counts,
    image_lo,
    image_hi,
    gate,
):
    img_rows, model_width = image_token_rows.shape
    local_heads = key_matrix.shape[1] // HEAD_SIZE
    flags = text_flags(image_lo, image_hi)
    gate_row = jnp.broadcast_to(gate[:, None], (1, HEAD_SIZE))
    group = lax.axis_index("group")
    core = lax.axis_index("head")
    index = lax.axis_index("seq")

    def head_weights(head):
        at = slice(head * HEAD_SIZE, (head + 1) * HEAD_SIZE)
        return jnp.concatenate([key_matrix[:, at], value_matrix[:, at]], axis=1)

    out = None
    if seq_size != 8 or img_rows % 32 or lax.axis_size("group") != 2:
        info = jnp.concatenate([image_counts, jnp.zeros((1,), jnp.int32)])
        for head in range(local_heads):
            weights = lax.all_gather(head_weights(head), "seq", axis=0, tiled=True)
            total = jnp.dot(image_token_rows, weights, preferred_element_type=jnp.float32)
            kv = lax.all_gather(finish(total, k_gain), "seq", axis=0, tiled=True)
            out = attend(queries, flags, gate_row, [kv], info, head, out)
        return out

    near = 2
    far = seq_size // near
    mine_far, mine_near = index // near, index % near
    shards = jnp.stack(
        [((mine_far - k) % far) * near + (mine_near ^ b) for k in range(far) for b in range(near)]
    ).astype(jnp.int32)
    info = jnp.concatenate([image_counts, shards])
    width = model_width // seq_size // 2
    across = [(0, 1), (1, 0)]
    chunks = 2
    each = seq_size // 2 // chunks
    direct = []
    for a in range(chunks):
        slots = lax.dynamic_slice_in_dim(shards, core * (seq_size // 2) + a * each, each)
        block = pick_blocks(2 * slots + (1 - group), image_token_rows, width)
        direct.append(lax.ppermute(block, "group", across))
    parts = [
        lax.dynamic_slice_in_dim(head_weights(head), group * width, width)
        for head in range(local_heads)
    ]
    spreads = []
    hold = ()
    for part in parts:
        pieces = spread(part, far, near, hold)
        hold = (pieces[2], pieces[2 * (far - 1)])
        spreads.append(pieces)
    passed = []
    for a in range(chunks):
        late = spreads[0] if a == 0 else spreads[min(1, local_heads - 1)][2:4]
        block = after(direct[a], *late) if ORDER else direct[a]
        passed.append(lax.ppermute(block, "head", across))
    own_blocks = 2 * shards + group
    core_arg = core.reshape(1).astype(jnp.int32)
    heads_kv = []
    for head in range(local_heads):
        weights = spreads[head]
        own = project_own(own_blocks, image_token_rows, weights, width)
        other = project_other(core_arg, direct, passed, weights)
        total = own + lax.ppermute(other, "group", across)
        heads_kv.append(spread(finish(total, k_gain), far, near))
    for head in range(local_heads):
        out = attend(queries, flags, gate_row, heads_kv[head], info, head, out)
    return out


def solution(mesh):
    in_specs = (
        P(("group", "seq"), "head"),
        P(("group", "seq"), None),
        P("seq", "head"),
        P("seq", "head"),
        P(),
        P("group"),
        P(("group", "seq")),
        P(("group", "seq")),
        P(),
    )
    out_specs = P(("group", "seq"), "head")
    return jax.shard_map(
        functools.partial(per_device, mesh.shape["seq"]),
        mesh=mesh,
        in_specs=in_specs,
        out_specs=out_specs,
        check_vma=False,
    )
```

```python
import functools
import math

import jax
import jax.numpy as jnp
from jax import lax
from jax.experimental import pallas as pl
from jax.experimental.pallas import tpu as pltpu
from jax.sharding import PartitionSpec as P

HEAD_SIZE = 128
QUERY_GROUP = 8
SLOT = 1664
NIMG = 2
CHUNK = 256
HEADS_AT_ONCE = 4
BIG = 2.0**98


def attention_kernel(slots, info, q_ref, flag_ref, gate_ref, *refs):
    kv_refs = refs[:slots]
    o_ref, keys, vals, *buffers = refs[-5:]
    piece = kv_refs[0].shape[0]
    rows = slots * piece

    @pl.when(pl.program_id(0) == 0)
    def _():
        lane = lax.broadcasted_iota(jnp.int32, (piece, HEAD_SIZE), 1)
        row = lax.broadcasted_iota(jnp.int32, (piece, HEAD_SIZE), 0)
        ones = jnp.where(lane == 0, 1.0, 0.0).astype(jnp.bfloat16)
        for j, kv_ref in enumerate(kv_refs):
            at = slice(j * piece, (j + 1) * piece)
            position = row + info[NIMG + j] * piece
            flags = jnp.zeros((piece, HEAD_SIZE), jnp.float32)
            for i in range(NIMG):
                mine = (position >= i * SLOT) & (position < (i + 1) * SLOT)
                beyond = mine & (position - i * SLOT >= info[i])
                hit = (mine & (lane == i)) | (beyond & (lane == NIMG))
                flags = jnp.where(hit, -BIG, flags)
            keys[at, :HEAD_SIZE] = kv_ref[:, :HEAD_SIZE]
            keys[at, HEAD_SIZE:] = flags.astype(jnp.bfloat16)
            vals[at, :HEAD_SIZE] = kv_ref[:, HEAD_SIZE:]
            vals[at, HEAD_SIZE:] = ones

    scale = math.log2(math.e) / math.sqrt(HEAD_SIZE)
    gain = jnp.tanh(gate_ref[...])
    top = None
    for i in range(HEADS_AT_ONCE + 1):
        now, later = buffers[(i + 1) % 2], buffers[i % 2]
        highest = total = None
        if i < HEADS_AT_ONCE:
            at = slice(i * HEAD_SIZE, (i + 1) * HEAD_SIZE)
            wide = jnp.concatenate([q_ref[:, at], flag_ref[...]], axis=1)
        for start in range(0, rows, CHUNK):
            chunk = slice(start, start + CHUNK)
            if i < HEADS_AT_ONCE:
                part = lax.dot_general(
                    wide,
                    keys[chunk, :],
                    (((1,), (1,)), ((), ())),
                    preferred_element_type=jnp.float32,
                )
                later[:, chunk] = part
                best = jnp.maximum(part[:, :HEAD_SIZE], part[:, HEAD_SIZE:])
                highest = best if highest is None else jnp.maximum(highest, best)
            if i > 0:
                weights = jnp.exp2((now[:, chunk] - top) * scale).astype(jnp.bfloat16)
                term = jnp.dot(weights, vals[chunk, :], preferred_element_type=jnp.float32)
                total = term if total is None else total + term
        if i > 0:
            at = slice((i - 1) * HEAD_SIZE, i * HEAD_SIZE)
            out = gain * (total[:, :HEAD_SIZE] / total[:, HEAD_SIZE : HEAD_SIZE + 1])
            o_ref[:, at] = out.astype(o_ref.dtype)
        if i < HEADS_AT_ONCE:
            top = jnp.max(highest, axis=1, keepdims=True)


def attend(queries, flags, gate_row, pieces, info, head, previous):
    text_rows, width = queries.shape
    slots = len(pieces)
    piece = pieces[0].shape[0]
    rows = slots * piece
    steps = QUERY_GROUP // HEADS_AT_ONCE
    block = HEADS_AT_ONCE * HEAD_SIZE
    grid_spec = pltpu.PrefetchScalarGridSpec(
        num_scalar_prefetch=1,
        grid=(steps,),
        in_specs=[
            pl.BlockSpec((text_rows, block), lambda g, s: (0, head * steps + g)),
            pl.BlockSpec((text_rows, HEAD_SIZE), lambda g, s: (0, 0)),
            pl.BlockSpec((1, HEAD_SIZE), lambda g, s: (0, 0)),
        ]
        + [pl.BlockSpec((piece, 2 * HEAD_SIZE), lambda g, s: (0, 0))] * slots
        + ([] if previous is None else [pl.BlockSpec(memory_space=pl.ANY)]),
        out_specs=pl.BlockSpec((text_rows, block), lambda g, s: (0, head * steps + g)),
        scratch_shapes=[
            pltpu.VMEM((rows, 2 * HEAD_SIZE), jnp.bfloat16),
            pltpu.VMEM((rows, 2 * HEAD_SIZE), jnp.bfloat16),
            pltpu.VMEM((text_rows, rows), jnp.float32),
            pltpu.VMEM((text_rows, rows), jnp.float32),
        ],
    )
    args = (info, queries, flags, gate_row, *pieces)
    aliases = {}
    if previous is not None:
        aliases = {len(args): 0}
        args = args + (previous,)
    return pl.pallas_call(
        functools.partial(attention_kernel, slots),
        out_shape=jax.ShapeDtypeStruct((text_rows, width), jnp.bfloat16),
        grid_spec=grid_spec,
        input_output_aliases=aliases,
        compiler_params=pltpu.CompilerParams(vmem_limit_bytes=40 * 2**20),
        cost_estimate=pl.CostEstimate(
            flops=8 * QUERY_GROUP * text_rows * rows * HEAD_SIZE,
            bytes_accessed=2 * rows * 2 * HEAD_SIZE,
            transcendentals=QUERY_GROUP * text_rows * rows,
        ),
    )(*args)


def text_flags(image_lo, image_hi):
    lane = jnp.arange(HEAD_SIZE)[None, :]
    hidden = (lane < NIMG) & ((lane < image_lo[:, None]) | (lane >= image_hi[:, None]))
    return (hidden | (lane == NIMG)).astype(jnp.bfloat16)


def pick_blocks(which, image, width):
    rows = image.shape[0]
    count = which.shape[0]

    def kernel(which_ref, image_ref, o_ref, sems):
        copies = []
        for j in range(count):
            column = pl.multiple_of(which_ref[j] * width, width)
            copies.append(
                pltpu.make_async_copy(image_ref.at[:, pl.ds(column, width)], o_ref.at[j], sems.at[j])
            )
        for copy in copies:
            copy.start()
        for copy in copies:
            copy.wait()

    return pl.pallas_call(
        kernel,
        out_shape=jax.ShapeDtypeStruct((count, rows, width), image.dtype),
        grid_spec=pltpu.PrefetchScalarGridSpec(
            num_scalar_prefetch=1,
            grid=(),
            in_specs=[pl.BlockSpec(memory_space=pl.ANY)],
            out_specs=pl.BlockSpec(memory_space=pltpu.VMEM),
            scratch_shapes=[pltpu.SemaphoreType.DMA((count,))],
        ),
        cost_estimate=pl.CostEstimate(
            flops=0, bytes_accessed=4 * count * rows * width, transcendentals=0
        ),
    )(which, image)


def project_own(which, image, weights, width):
    rows = image.shape[0]
    count = len(weights)
    columns = weights[0].shape[1]
    half = rows // 2

    def kernel(which_ref, *refs):
        total = None
        for j in range(count):
            term = jnp.dot(
                refs[j][...], refs[count + j][...], preferred_element_type=jnp.float32
            )
            total = term if total is None else total + term
        refs[-1][...] = total

    def block_of(j):
        return pl.BlockSpec((half, width), lambda i, which: (i, which[j]))

    return pl.pallas_call(
        kernel,
        out_shape=jax.ShapeDtypeStruct((rows, columns), jnp.float32),
        grid_spec=pltpu.PrefetchScalarGridSpec(
            num_scalar_prefetch=1,
            grid=(2,),
            in_specs=[block_of(j) for j in range(count)]
            + [pl.BlockSpec((width, columns), lambda i, which: (0, 0))] * count,
            out_specs=pl.BlockSpec((half, columns), lambda i, which: (i, 0)),
        ),
        compiler_params=pltpu.CompilerParams(vmem_limit_bytes=32 * 2**20),
        cost_estimate=pl.CostEstimate(
            flops=2 * count * rows * width * columns,
            bytes_accessed=2 * count * width * (rows + columns),
            transcendentals=0,
        ),
    )(which, *([image] * count), *weights)


def project_other(core, direct, passed, weights):
    each, rows, width = direct[0].shape
    chunks = len(direct)
    count = len(weights)
    columns = weights[0].shape[1]
    half = rows // 2

    def kernel(core_ref, *refs):
        direct_refs = refs[:chunks]
        passed_refs = refs[chunks : 2 * chunks]
        weight_refs = refs[2 * chunks : 2 * chunks + count]

        def run(first, second):
            total = None
            for start, group in ((0, first), (count // 2, second)):
                for a in range(chunks):
                    for i in range(each):
                        term = jnp.dot(
                            group[a][i],
                            weight_refs[start + a * each + i][...],
                            preferred_element_type=jnp.float32,
                        )
                        total = term if total is None else total + term
            refs[-1][...] = total

        @pl.when(core_ref[0] == 0)
        def _():
            run(direct_refs, passed_refs)

        @pl.when(core_ref[0] != 0)
        def _():
            run(passed_refs, direct_refs)

    return pl.pallas_call(
        kernel,
        out_shape=jax.ShapeDtypeStruct((rows, columns), jnp.float32),
        grid_spec=pltpu.PrefetchScalarGridSpec(
            num_scalar_prefetch=1,
            grid=(2,),
            in_specs=[pl.BlockSpec((each, half, width), lambda i, core: (0, i, 0))] * (2 * chunks)
            + [pl.BlockSpec((width, columns), lambda i, core: (0, 0))] * count,
            out_specs=pl.BlockSpec((half, columns), lambda i, core: (i, 0)),
        ),
        compiler_params=pltpu.CompilerParams(vmem_limit_bytes=32 * 2**20),
        cost_estimate=pl.CostEstimate(
            flops=2 * count * rows * width * columns,
            bytes_accessed=2 * count * width * (rows + columns),
            transcendentals=0,
        ),
    )(core, *direct, *passed, *weights)


def after(value, *others):
    return lax.optimization_barrier((value, *others))[0]


def swap(value, size):
    return lax.ppermute(value, "seq", [(i, i ^ 1) for i in range(size)])


def shift(value, far, near, step):
    pairs = [(f * near + n, ((f + step) % far) * near + n) for f in range(far) for n in range(near)]
    return lax.ppermute(value, "seq", pairs)


def finish(total, k_gain):
    key_head = total[:, :HEAD_SIZE]
    inverse = lax.rsqrt(jnp.mean(key_head * key_head, axis=-1, keepdims=True) + 1e-05)
    key_head = (key_head * inverse * k_gain).astype(jnp.bfloat16)
    return jnp.concatenate([key_head, total[:, HEAD_SIZE:].astype(jnp.bfloat16)], axis=1)


def per_device(
    seq_size,
    queries,
    image_token_rows,
    key_matrix,
    value_matrix,
    k_gain,
    image_counts,
    image_lo,
    image_hi,
    gate,
):
    img_rows, model_width = image_token_rows.shape
    local_heads = key_matrix.shape[1] // HEAD_SIZE
    flags = text_flags(image_lo, image_hi)
    gate_row = jnp.broadcast_to(gate[:, None], (1, HEAD_SIZE))
    group = lax.axis_index("group")
    core = lax.axis_index("head")
    index = lax.axis_index("seq")

    def head_weights(head):
        at = slice(head * HEAD_SIZE, (head + 1) * HEAD_SIZE)
        return jnp.concatenate([key_matrix[:, at], value_matrix[:, at]], axis=1)

    out = None
    if (seq_size, local_heads) != (8, 2) or img_rows % 32 or lax.axis_size("group") != 2:
        info = jnp.concatenate([image_counts, jnp.zeros((1,), jnp.int32)])
        for head in range(local_heads):
            weights = lax.all_gather(head_weights(head), "seq", axis=0, tiled=True)
            total = jnp.dot(image_token_rows, weights, preferred_element_type=jnp.float32)
            kv = lax.all_gather(finish(total, k_gain), "seq", axis=0, tiled=True)
            out = attend(queries, flags, gate_row, [kv], info, head, out)
        return out

    near = 2
    far = seq_size // near
    mine_far, mine_near = index // near, index % near
    shards = jnp.stack(
        [((mine_far - k) % far) * near + (mine_near ^ b) for k in range(far) for b in range(near)]
    ).astype(jnp.int32)
    info = jnp.concatenate([image_counts, shards])
    width = model_width // seq_size // 2
    across = [(0, 1), (1, 0)]
    chunks = 1
    each = seq_size // 2 // chunks
    direct = []
    for a in range(chunks):
        slots = lax.dynamic_slice_in_dim(shards, core * (seq_size // 2) + a * each, each)
        block = pick_blocks(2 * slots + (1 - group), image_token_rows, width)
        direct.append(lax.ppermute(block, "group", across))
    parts = [
        lax.dynamic_slice_in_dim(head_weights(head), group * width, width)
        for head in range(local_heads)
    ]
    size = seq_size
    w0, w1 = parts
    a1, a3 = shift(w0, far, near, 1), shift(w0, far, near, 3)
    a0x, b0x = swap(w0, size), swap(w1, size)
    a2 = shift(after(a1, a3), far, near, 1)
    a1x = swap(after(a1, a3), size)
    a3x = swap(after(a3, a0x, b0x), size)
    b1 = shift(after(w1, a3, a0x, b0x), far, near, 1)
    a2x = swap(a2, size)
    b3 = shift(after(w1, a1x), far, near, 3)
    b2 = shift(b1, far, near, 1)
    b1x = shift(after(b0x, a3x), far, near, 1)
    b3x = swap(b3, size)
    passed = [
        lax.ppermute(after(block, a1x, a3x, a2x, b1, b3), "head", across) for block in direct
    ]
    b2x = swap(after(b2, *passed), size)
    spreads = [[w0, a0x, a1, a1x, a2, a2x, a3, a3x], [w1, b0x, b1, b1x, b2, b2x, b3, b3x]]
    own_blocks = 2 * shards + group
    core_arg = core.reshape(1).astype(jnp.int32)
    others, owns = [], []
    for weights in spreads:
        others.append(project_other(core_arg, direct, passed, after(weights, *others[-1:])))
        owns.append(project_own(own_blocks, image_token_rows, weights, width))
    k0 = finish(owns[0] + lax.ppermute(others[0], "group", across), k_gain)
    a1, a3, a0x = shift(k0, far, near, 1), shift(k0, far, near, 3), swap(k0, size)
    k1 = finish(owns[1] + after(lax.ppermute(others[1], "group", across), a0x), k_gain)
    a2 = shift(a1, far, near, 1)
    a1x, a3x = swap(a1, size), swap(a3, size)
    b0x = swap(k1, size)
    b1 = shift(after(k1, a1, a3), far, near, 1)
    b3 = shift(after(k1, a1, a3), far, near, 3)
    a2x = swap(a2, size)
    b2 = shift(b1, far, near, 1)
    b1x = shift(after(b0x, a3x), far, near, 1)
    b3x = swap(b3, size)
    b2x = swap(b2, size)
    heads_kv = [[k0, a0x, a1, a1x, a2, a2x, a3, a3x], [k1, b0x, b1, b1x, b2, b2x, b3, b3x]]
    for head in range(local_heads):
        out = attend(queries, flags, gate_row, heads_kv[head], info, head, out)
    return out


def solution(mesh):
    in_specs = (
        P(("group", "seq"), "head"),
        P(("group", "seq"), None),
        P("seq", "head"),
        P("seq", "head"),
        P(),
        P("group"),
        P(("group", "seq")),
        P(("group", "seq")),
        P(),
    )
    out_specs = P(("group", "seq"), "head")
    return jax.shard_map(
        functools.partial(per_device, mesh.shape["seq"]),
        mesh=mesh,
        in_specs=in_specs,
        out_specs=out_specs,
        check_vma=False,
    )
```

```python
import functools
import math

import jax
import jax.numpy as jnp
from jax import lax
from jax.experimental import pallas as pl
from jax.experimental.pallas import tpu as pltpu
from jax.sharding import PartitionSpec as P

HEAD_SIZE = 128
QUERY_GROUP = 8
SLOT = 1664
NIMG = 2
CHUNK = 256
HEADS_AT_ONCE = 4
BIG = 2.0**98


def attention_kernel(slots, resumed, last, info, q_ref, flag_ref, gate_ref, *refs):
    kv_refs = refs[:slots]
    o_ref, keys, vals, *buffers = refs[-5:]
    state_ref = refs[slots] if resumed else None
    piece = kv_refs[0].shape[0]
    rows = slots * piece

    @pl.when(pl.program_id(0) == 0)
    def _():
        lane = lax.broadcasted_iota(jnp.int32, (piece, HEAD_SIZE), 1)
        row = lax.broadcasted_iota(jnp.int32, (piece, HEAD_SIZE), 0)
        ones = jnp.where(lane == 0, 1.0, 0.0).astype(jnp.bfloat16)
        for j, kv_ref in enumerate(kv_refs):
            at = slice(j * piece, (j + 1) * piece)
            position = row + info[NIMG + j] * piece
            flags = jnp.zeros((piece, HEAD_SIZE), jnp.float32)
            for i in range(NIMG):
                mine = (position >= i * SLOT) & (position < (i + 1) * SLOT)
                beyond = mine & (position - i * SLOT >= info[i])
                hit = (mine & (lane == i)) | (beyond & (lane == NIMG))
                flags = jnp.where(hit, -BIG, flags)
            keys[at, :HEAD_SIZE] = kv_ref[:, :HEAD_SIZE]
            keys[at, HEAD_SIZE:] = flags.astype(jnp.bfloat16)
            vals[at, :HEAD_SIZE] = kv_ref[:, HEAD_SIZE:]
            vals[at, HEAD_SIZE:] = ones

    scale = math.log2(math.e) / math.sqrt(HEAD_SIZE)
    gain = jnp.tanh(gate_ref[...])
    top = None
    for i in range(HEADS_AT_ONCE + 1):
        now, later = buffers[(i + 1) % 2], buffers[i % 2]
        highest = total = None
        if i < HEADS_AT_ONCE:
            at = slice(i * HEAD_SIZE, (i + 1) * HEAD_SIZE)
            wide = jnp.concatenate([q_ref[:, at], flag_ref[...]], axis=1)
        for start in range(0, rows, CHUNK):
            chunk = slice(start, min(start + CHUNK, rows))
            if i < HEADS_AT_ONCE:
                part = lax.dot_general(
                    wide,
                    keys[chunk, :],
                    (((1,), (1,)), ((), ())),
                    preferred_element_type=jnp.float32,
                )
                later[:, chunk] = part
                for lane in range(0, part.shape[1], HEAD_SIZE):
                    best = part[:, lane : lane + HEAD_SIZE]
                    highest = best if highest is None else jnp.maximum(highest, best)
            if i > 0:
                weights = jnp.exp2((now[:, chunk] - top) * scale).astype(jnp.bfloat16)
                term = jnp.dot(weights, vals[chunk, :], preferred_element_type=jnp.float32)
                total = term if total is None else total + term
        if i > 0:
            g = i - 1
            if resumed:
                before = state_ref[:, g * 2 * HEAD_SIZE : (g + 1) * 2 * HEAD_SIZE]
                total = total + before * jnp.exp2((before_top - top) * scale)
            if last:
                at = slice(g * HEAD_SIZE, (g + 1) * HEAD_SIZE)
                out = gain * (total[:, :HEAD_SIZE] / total[:, HEAD_SIZE : HEAD_SIZE + 1])
                o_ref[:, at] = out.astype(o_ref.dtype)
            else:
                at = g * 2 * HEAD_SIZE
                lane = lax.broadcasted_iota(jnp.int32, (total.shape[0], HEAD_SIZE), 1)
                o_ref[:, at : at + HEAD_SIZE] = total[:, :HEAD_SIZE]
                o_ref[:, at + HEAD_SIZE : at + 2 * HEAD_SIZE] = jnp.where(
                    lane == 1, top, total[:, HEAD_SIZE:]
                )
        if i < HEADS_AT_ONCE:
            top = jnp.max(highest, axis=1, keepdims=True)
            if resumed:
                at = i * 2 * HEAD_SIZE + HEAD_SIZE + 1
                before_top = state_ref[:, at : at + 1]
                top = jnp.maximum(top, before_top)


def attend(queries, flags, gate_row, pieces, info, head, previous, state=None, last=True):
    text_rows, width = queries.shape
    slots = len(pieces)
    piece = pieces[0].shape[0]
    rows = slots * piece
    steps = QUERY_GROUP // HEADS_AT_ONCE
    block = HEADS_AT_ONCE * HEAD_SIZE
    state_spec = pl.BlockSpec((text_rows, 2 * block), lambda g, s: (0, g))
    if last:
        out_spec = pl.BlockSpec((text_rows, block), lambda g, s: (0, head * steps + g))
        out_shape = jax.ShapeDtypeStruct((text_rows, width), jnp.bfloat16)
    else:
        out_spec = state_spec
        out_shape = jax.ShapeDtypeStruct((text_rows, 2 * QUERY_GROUP * HEAD_SIZE), jnp.float32)
    in_specs = [
        pl.BlockSpec((text_rows, block), lambda g, s: (0, head * steps + g)),
        pl.BlockSpec((text_rows, HEAD_SIZE), lambda g, s: (0, 0)),
        pl.BlockSpec((1, HEAD_SIZE), lambda g, s: (0, 0)),
    ] + [pl.BlockSpec(memory_space=pltpu.VMEM)] * slots
    args = [info, queries, flags, gate_row, *pieces]
    if state is not None:
        in_specs.append(state_spec)
        args.append(state)
    aliases = {}
    if previous is not None:
        in_specs.append(pl.BlockSpec(memory_space=pl.ANY))
        aliases = {len(args): 0}
        args.append(previous)
    return pl.pallas_call(
        functools.partial(attention_kernel, slots, state is not None, last),
        out_shape=out_shape,
        grid_spec=pltpu.PrefetchScalarGridSpec(
            num_scalar_prefetch=1,
            grid=(steps,),
            in_specs=in_specs,
            out_specs=out_spec,
            scratch_shapes=[
                pltpu.VMEM((rows, 2 * HEAD_SIZE), jnp.bfloat16),
                pltpu.VMEM((rows, 2 * HEAD_SIZE), jnp.bfloat16),
                pltpu.VMEM((text_rows, rows), jnp.float32),
                pltpu.VMEM((text_rows, rows), jnp.float32),
            ],
        ),
        input_output_aliases=aliases,
        compiler_params=pltpu.CompilerParams(vmem_limit_bytes=40 * 2**20),
        cost_estimate=pl.CostEstimate(
            flops=8 * QUERY_GROUP * text_rows * rows * HEAD_SIZE,
            bytes_accessed=2 * rows * 2 * HEAD_SIZE,
            transcendentals=QUERY_GROUP * text_rows * rows,
        ),
    )(*args)


def text_flags(image_lo, image_hi):
    lane = jnp.arange(HEAD_SIZE)[None, :]
    hidden = (lane < NIMG) & ((lane < image_lo[:, None]) | (lane >= image_hi[:, None]))
    return (hidden | (lane == NIMG)).astype(jnp.bfloat16)


def pick_blocks(which, image, width):
    rows = image.shape[0]
    count = which.shape[0]

    def kernel(which_ref, image_ref, o_ref, sems):
        copies = []
        for j in range(count):
            column = pl.multiple_of(which_ref[j] * width, width)
            copies.append(
                pltpu.make_async_copy(image_ref.at[:, pl.ds(column, width)], o_ref.at[j], sems.at[j])
            )
        for copy in copies:
            copy.start()
        for copy in copies:
            copy.wait()

    return pl.pallas_call(
        kernel,
        out_shape=jax.ShapeDtypeStruct((count, rows, width), image.dtype),
        grid_spec=pltpu.PrefetchScalarGridSpec(
            num_scalar_prefetch=1,
            grid=(),
            in_specs=[pl.BlockSpec(memory_space=pl.ANY)],
            out_specs=pl.BlockSpec(memory_space=pltpu.VMEM),
            scratch_shapes=[pltpu.SemaphoreType.DMA((count,))],
        ),
        cost_estimate=pl.CostEstimate(
            flops=0, bytes_accessed=4 * count * rows * width, transcendentals=0
        ),
    )(which, image)


def project_own(which, image, weights, width):
    rows = image.shape[0]
    count = len(weights)
    columns = weights[0].shape[1]
    half = rows // 2

    def kernel(which_ref, *refs):
        total = None
        for j in range(count):
            term = jnp.dot(
                refs[j][...], refs[count + j][...], preferred_element_type=jnp.float32
            )
            total = term if total is None else total + term
        refs[-1][...] = total

    def block_of(j):
        return pl.BlockSpec((half, width), lambda i, which: (i, which[j]))

    return pl.pallas_call(
        kernel,
        out_shape=jax.ShapeDtypeStruct((rows, columns), jnp.float32),
        grid_spec=pltpu.PrefetchScalarGridSpec(
            num_scalar_prefetch=1,
            grid=(2,),
            in_specs=[block_of(j) for j in range(count)]
            + [pl.BlockSpec((width, columns), lambda i, which: (0, 0))] * count,
            out_specs=pl.BlockSpec((half, columns), lambda i, which: (i, 0)),
        ),
        compiler_params=pltpu.CompilerParams(vmem_limit_bytes=32 * 2**20),
        cost_estimate=pl.CostEstimate(
            flops=2 * count * rows * width * columns,
            bytes_accessed=2 * count * width * (rows + columns),
            transcendentals=0,
        ),
    )(which, *([image] * count), *weights)


def project_other(core, direct, passed, weights):
    each, rows, width = direct[0].shape
    chunks = len(direct)
    count = len(weights)
    columns = weights[0].shape[1]
    half = rows // 2

    def kernel(core_ref, *refs):
        direct_refs = refs[:chunks]
        passed_refs = refs[chunks : 2 * chunks]
        weight_refs = refs[2 * chunks : 2 * chunks + count]

        def run(first, second):
            total = None
            for start, group in ((0, first), (count // 2, second)):
                for a in range(chunks):
                    for i in range(each):
                        term = jnp.dot(
                            group[a][i],
                            weight_refs[start + a * each + i][...],
                            preferred_element_type=jnp.float32,
                        )
                        total = term if total is None else total + term
            refs[-1][...] = total

        @pl.when(core_ref[0] == 0)
        def _():
            run(direct_refs, passed_refs)

        @pl.when(core_ref[0] != 0)
        def _():
            run(passed_refs, direct_refs)

    return pl.pallas_call(
        kernel,
        out_shape=jax.ShapeDtypeStruct((rows, columns), jnp.float32),
        grid_spec=pltpu.PrefetchScalarGridSpec(
            num_scalar_prefetch=1,
            grid=(2,),
            in_specs=[pl.BlockSpec((each, half, width), lambda i, core: (0, i, 0))] * (2 * chunks)
            + [pl.BlockSpec((width, columns), lambda i, core: (0, 0))] * count,
            out_specs=pl.BlockSpec((half, columns), lambda i, core: (i, 0)),
        ),
        compiler_params=pltpu.CompilerParams(vmem_limit_bytes=32 * 2**20),
        cost_estimate=pl.CostEstimate(
            flops=2 * count * rows * width * columns,
            bytes_accessed=2 * count * width * (rows + columns),
            transcendentals=0,
        ),
    )(core, *direct, *passed, *weights)


def after(value, *others):
    return lax.optimization_barrier((value, *others))[0]


def swap(value, size):
    return lax.ppermute(value, "seq", [(i, i ^ 1) for i in range(size)])


def shift(value, far, near, step):
    pairs = [(f * near + n, ((f + step) % far) * near + n) for f in range(far) for n in range(near)]
    return lax.ppermute(value, "seq", pairs)


def finish(total, k_gain):
    key_head = total[:, :HEAD_SIZE]
    inverse = lax.rsqrt(jnp.mean(key_head * key_head, axis=-1, keepdims=True) + 1e-05)
    key_head = (key_head * inverse * k_gain).astype(jnp.bfloat16)
    return jnp.concatenate([key_head, total[:, HEAD_SIZE:].astype(jnp.bfloat16)], axis=1)


def per_device(
    seq_size,
    queries,
    image_token_rows,
    key_matrix,
    value_matrix,
    k_gain,
    image_counts,
    image_lo,
    image_hi,
    gate,
):
    img_rows, model_width = image_token_rows.shape
    local_heads = key_matrix.shape[1] // HEAD_SIZE
    flags = text_flags(image_lo, image_hi)
    gate_row = jnp.broadcast_to(gate[:, None], (1, HEAD_SIZE))
    group = lax.axis_index("group")
    core = lax.axis_index("head")
    index = lax.axis_index("seq")

    def head_weights(head):
        at = slice(head * HEAD_SIZE, (head + 1) * HEAD_SIZE)
        return jnp.concatenate([key_matrix[:, at], value_matrix[:, at]], axis=1)

    out = None
    if (seq_size, local_heads) != (8, 2) or img_rows % 32 or lax.axis_size("group") != 2:
        info = jnp.concatenate([image_counts, jnp.zeros((1,), jnp.int32)])
        for head in range(local_heads):
            weights = lax.all_gather(head_weights(head), "seq", axis=0, tiled=True)
            total = jnp.dot(image_token_rows, weights, preferred_element_type=jnp.float32)
            kv = lax.all_gather(finish(total, k_gain), "seq", axis=0, tiled=True)
            out = attend(queries, flags, gate_row, [kv], info, head, out)
        return out

    near = 2
    far = seq_size // near
    mine_far, mine_near = index // near, index % near
    shards = jnp.stack(
        [((mine_far - k) % far) * near + (mine_near ^ b) for k in range(far) for b in range(near)]
    ).astype(jnp.int32)
    width = model_width // seq_size // 2
    across = [(0, 1), (1, 0)]
    chunks = 1
    each = seq_size // 2 // chunks
    direct = []
    for a in range(chunks):
        slots = lax.dynamic_slice_in_dim(shards, core * (seq_size // 2) + a * each, each)
        block = pick_blocks(2 * slots + (1 - group), image_token_rows, width)
        direct.append(lax.ppermute(block, "group", across))
    parts = [
        lax.dynamic_slice_in_dim(head_weights(head), group * width, width)
        for head in range(local_heads)
    ]
    size = seq_size
    w0, w1 = parts
    a1, a3 = shift(w0, far, near, 1), shift(w0, far, near, 3)
    a0x, b0x = swap(w0, size), swap(w1, size)
    a2 = shift(after(a1, a3), far, near, 1)
    a1x = swap(after(a1, a3), size)
    a3x = swap(after(a3, a0x, b0x), size)
    b1 = shift(after(w1, a3, a0x, b0x), far, near, 1)
    a2x = swap(a2, size)
    b3 = shift(after(w1, a1x), far, near, 3)
    b2 = shift(b1, far, near, 1)
    b1x = shift(after(b0x, a3x), far, near, 1)
    b3x = swap(b3, size)
    passed = [
        lax.ppermute(after(block, a1x, a3x, a2x, b1, b3), "head", across) for block in direct
    ]
    b2x = swap(b2, size)
    spreads = [[w0, a0x, a1, a1x, a2, a2x, a3, a3x], [w1, b0x, b1, b1x, b2, b2x, b3, b3x]]
    own_blocks = 2 * shards + group
    core_arg = core.reshape(1).astype(jnp.int32)
    own0 = project_own(own_blocks, image_token_rows, spreads[0], width)
    other0 = project_other(core_arg, direct, passed, after(spreads[0], own0))
    k0 = finish(own0 + lax.ppermute(other0, "group", across), k_gain)
    weights1 = after(spreads[1], k0)
    other1 = project_other(core_arg, direct, passed, weights1)
    own1 = project_own(own_blocks, image_token_rows, weights1, width)
    a1, a3, a0x = shift(k0, far, near, 1), shift(k0, far, near, 3), swap(k0, size)
    k1 = finish(own1 + after(lax.ppermute(other1, "group", across), a0x), k_gain)

    def part(head, slots, pieces, previous=None, state=None, last=True):
        here = jnp.concatenate([image_counts, jnp.stack([shards[j] for j in slots])])
        return attend(queries, flags, gate_row, pieces, here, head, previous, state, last)

    a2 = shift(a1, far, near, 1)
    a1x, a3x = swap(a1, size), swap(a3, size)
    b0x = swap(k1, size)
    b1 = shift(after(k1, a1, a3), far, near, 1)
    b3 = shift(after(k1, a1, a3), far, near, 3)
    state = part(0, (0, 1, 2, 6), [k0, a0x, a1, a3], last=False)
    a2x = swap(a2, size)
    b2 = shift(b1, far, near, 1)
    b1x = shift(after(b0x, a3x), far, near, 1)
    b3x = swap(b3, size)
    b2x = swap(after(b2, state), size)
    out = part(0, (3, 7, 4, 5), [a1x, a3x, a2, a2x], state=state)
    state = part(1, (0, 1, 2, 6), [k1, b0x, b1, b3], last=False)
    return part(1, (3, 7, 4, 5), [b1x, b3x, b2, b2x], out, state)


def solution(mesh):
    in_specs = (
        P(("group", "seq"), "head"),
        P(("group", "seq"), None),
        P("seq", "head"),
        P("seq", "head"),
        P(),
        P("group"),
        P(("group", "seq")),
        P(("group", "seq")),
        P(),
    )
    out_specs = P(("group", "seq"), "head")
    return jax.shard_map(
        functools.partial(per_device, mesh.shape["seq"]),
        mesh=mesh,
        in_specs=in_specs,
        out_specs=out_specs,
        check_vma=False,
    )
```

```python
import functools
import math

import jax
import jax.numpy as jnp
from jax import lax
from jax.experimental import pallas as pl
from jax.experimental.pallas import tpu as pltpu
from jax.sharding import PartitionSpec as P

HEAD_SIZE = 128
QUERY_GROUP = 8
SLOT = 1664
NIMG = 2
CHUNK = 256
HEADS_AT_ONCE = 4
BIG = 2.0**98


def attention_kernel(slots, resumed, last, info, q_ref, flag_ref, gate_ref, *refs):
    kv_refs = refs[:slots]
    o_ref, keys, vals, *buffers = refs[-5:]
    state_ref = refs[slots] if resumed else None
    piece = kv_refs[0].shape[0]
    rows = slots * piece

    @pl.when(pl.program_id(0) == 0)
    def _():
        lane = lax.broadcasted_iota(jnp.int32, (piece, HEAD_SIZE), 1)
        row = lax.broadcasted_iota(jnp.int32, (piece, HEAD_SIZE), 0)
        ones = jnp.where(lane == 0, 1.0, 0.0).astype(jnp.bfloat16)
        for j, kv_ref in enumerate(kv_refs):
            at = slice(j * piece, (j + 1) * piece)
            position = row + info[NIMG + j] * piece
            flags = jnp.zeros((piece, HEAD_SIZE), jnp.float32)
            for i in range(NIMG):
                mine = (position >= i * SLOT) & (position < (i + 1) * SLOT)
                beyond = mine & (position - i * SLOT >= info[i])
                hit = (mine & (lane == i)) | (beyond & (lane == NIMG))
                flags = jnp.where(hit, -BIG, flags)
            keys[at, :HEAD_SIZE] = kv_ref[:, :HEAD_SIZE]
            keys[at, HEAD_SIZE:] = flags.astype(jnp.bfloat16)
            vals[at, :HEAD_SIZE] = kv_ref[:, HEAD_SIZE:]
            vals[at, HEAD_SIZE:] = ones

    scale = math.log2(math.e) / math.sqrt(HEAD_SIZE)
    gain = jnp.tanh(gate_ref[...])
    top = None
    for i in range(HEADS_AT_ONCE + 1):
        now, later = buffers[(i + 1) % 2], buffers[i % 2]
        highest = total = None
        if i < HEADS_AT_ONCE:
            at = slice(i * HEAD_SIZE, (i + 1) * HEAD_SIZE)
            wide = jnp.concatenate([q_ref[:, at], flag_ref[...]], axis=1)
        for start in range(0, rows, CHUNK):
            chunk = slice(start, min(start + CHUNK, rows))
            if i < HEADS_AT_ONCE:
                part = lax.dot_general(
                    wide,
                    keys[chunk, :],
                    (((1,), (1,)), ((), ())),
                    preferred_element_type=jnp.float32,
                )
                later[:, chunk] = part
                for lane in range(0, part.shape[1], HEAD_SIZE):
                    best = part[:, lane : lane + HEAD_SIZE]
                    highest = best if highest is None else jnp.maximum(highest, best)
            if i > 0:
                weights = jnp.exp2((now[:, chunk] - top) * scale).astype(jnp.bfloat16)
                term = jnp.dot(weights, vals[chunk, :], preferred_element_type=jnp.float32)
                total = term if total is None else total + term
        if i > 0:
            g = i - 1
            if resumed:
                before = state_ref[:, g * 2 * HEAD_SIZE : (g + 1) * 2 * HEAD_SIZE]
                total = total + before * jnp.exp2((before_top - top) * scale)
            if last:
                at = slice(g * HEAD_SIZE, (g + 1) * HEAD_SIZE)
                out = gain * (total[:, :HEAD_SIZE] / total[:, HEAD_SIZE : HEAD_SIZE + 1])
                o_ref[:, at] = out.astype(o_ref.dtype)
            else:
                at = g * 2 * HEAD_SIZE
                lane = lax.broadcasted_iota(jnp.int32, (total.shape[0], HEAD_SIZE), 1)
                o_ref[:, at : at + HEAD_SIZE] = total[:, :HEAD_SIZE]
                o_ref[:, at + HEAD_SIZE : at + 2 * HEAD_SIZE] = jnp.where(
                    lane == 1, top, total[:, HEAD_SIZE:]
                )
        if i < HEADS_AT_ONCE:
            top = jnp.max(highest, axis=1, keepdims=True)
            if resumed:
                at = i * 2 * HEAD_SIZE + HEAD_SIZE + 1
                before_top = state_ref[:, at : at + 1]
                top = jnp.maximum(top, before_top)


def attend(queries, flags, gate_row, pieces, info, head, previous, state=None, last=True):
    text_rows, width = queries.shape
    slots = len(pieces)
    piece = pieces[0].shape[0]
    rows = slots * piece
    steps = QUERY_GROUP // HEADS_AT_ONCE
    block = HEADS_AT_ONCE * HEAD_SIZE
    state_spec = pl.BlockSpec((text_rows, 2 * block), lambda g, s: (0, g))
    if last:
        out_spec = pl.BlockSpec((text_rows, block), lambda g, s: (0, head * steps + g))
        out_shape = jax.ShapeDtypeStruct((text_rows, width), jnp.bfloat16)
    else:
        out_spec = state_spec
        out_shape = jax.ShapeDtypeStruct((text_rows, 2 * QUERY_GROUP * HEAD_SIZE), jnp.float32)
    in_specs = [
        pl.BlockSpec((text_rows, block), lambda g, s: (0, head * steps + g)),
        pl.BlockSpec((text_rows, HEAD_SIZE), lambda g, s: (0, 0)),
        pl.BlockSpec((1, HEAD_SIZE), lambda g, s: (0, 0)),
    ] + [pl.BlockSpec(memory_space=pltpu.VMEM)] * slots
    args = [info, queries, flags, gate_row, *pieces]
    if state is not None:
        in_specs.append(state_spec)
        args.append(state)
    aliases = {}
    if previous is not None:
        in_specs.append(pl.BlockSpec(memory_space=pl.ANY))
        aliases = {len(args): 0}
        args.append(previous)
    return pl.pallas_call(
        functools.partial(attention_kernel, slots, state is not None, last),
        out_shape=out_shape,
        grid_spec=pltpu.PrefetchScalarGridSpec(
            num_scalar_prefetch=1,
            grid=(steps,),
            in_specs=in_specs,
            out_specs=out_spec,
            scratch_shapes=[
                pltpu.VMEM((rows, 2 * HEAD_SIZE), jnp.bfloat16),
                pltpu.VMEM((rows, 2 * HEAD_SIZE), jnp.bfloat16),
                pltpu.VMEM((text_rows, rows), jnp.float32),
                pltpu.VMEM((text_rows, rows), jnp.float32),
            ],
        ),
        input_output_aliases=aliases,
        compiler_params=pltpu.CompilerParams(vmem_limit_bytes=28 * 2**20),
        cost_estimate=pl.CostEstimate(
            flops=8 * QUERY_GROUP * text_rows * rows * HEAD_SIZE,
            bytes_accessed=2 * rows * 2 * HEAD_SIZE,
            transcendentals=QUERY_GROUP * text_rows * rows,
        ),
    )(*args)


def text_flags(image_lo, image_hi):
    lane = jnp.arange(HEAD_SIZE)[None, :]
    hidden = (lane < NIMG) & ((lane < image_lo[:, None]) | (lane >= image_hi[:, None]))
    return (hidden | (lane == NIMG)).astype(jnp.bfloat16)


def pick_blocks(which, image, width):
    rows = image.shape[0]
    count = which.shape[0]

    def kernel(which_ref, image_ref, o_ref, sems):
        copies = []
        for j in range(count):
            column = pl.multiple_of(which_ref[j] * width, width)
            copies.append(
                pltpu.make_async_copy(image_ref.at[:, pl.ds(column, width)], o_ref.at[j], sems.at[j])
            )
        for copy in copies:
            copy.start()
        for copy in copies:
            copy.wait()

    return pl.pallas_call(
        kernel,
        out_shape=jax.ShapeDtypeStruct((count, rows, width), image.dtype),
        grid_spec=pltpu.PrefetchScalarGridSpec(
            num_scalar_prefetch=1,
            grid=(),
            in_specs=[pl.BlockSpec(memory_space=pl.ANY)],
            out_specs=pl.BlockSpec(memory_space=pltpu.VMEM),
            scratch_shapes=[pltpu.SemaphoreType.DMA((count,))],
        ),
        compiler_params=pltpu.CompilerParams(vmem_limit_bytes=8 * 2**20),
        cost_estimate=pl.CostEstimate(
            flops=0, bytes_accessed=4 * count * rows * width, transcendentals=0
        ),
    )(which, image)


def in_vmem(count):
    return [pl.BlockSpec(memory_space=pltpu.VMEM)] * count


def dots(blocks, weights):
    total = None
    for block, weight in zip(blocks, weights):
        term = jnp.dot(block, weight[...], preferred_element_type=jnp.float32)
        total = term if total is None else total + term
    return total


def project(core, mine, direct, passed, weights):
    count, rows, width = mine.shape
    columns = weights[0].shape[1]

    def kernel(core_ref, mine_ref, direct_ref, passed_ref, *refs):
        other_ref, own_ref = refs[-2:]

        def run(*halves):
            blocks = [half[j] for half in halves for j in range(count // 2)]
            other_ref[...] = dots(blocks, refs[:count])

        @pl.when(core_ref[0] == 0)
        def _():
            run(direct_ref, passed_ref)

        @pl.when(core_ref[0] != 0)
        def _():
            run(passed_ref, direct_ref)

        own_ref[...] = dots([mine_ref[j] for j in range(count)], refs[:count])

    shape = jax.ShapeDtypeStruct((rows, columns), jnp.float32)
    return pl.pallas_call(
        kernel,
        out_shape=(shape, shape),
        in_specs=[pl.BlockSpec(memory_space=pltpu.SMEM)] + in_vmem(3 + count),
        out_specs=tuple(in_vmem(2)),
        compiler_params=pltpu.CompilerParams(vmem_limit_bytes=16 * 2**20),
        cost_estimate=pl.CostEstimate(
            flops=4 * count * rows * width * columns,
            bytes_accessed=4 * count * width * (rows + columns),
            transcendentals=0,
        ),
    )(core, mine, direct, passed, *weights)


def after(value, *others):
    return lax.optimization_barrier((value, *others))[0]


def swap(value, size):
    return lax.ppermute(value, "seq", [(i, i ^ 1) for i in range(size)])


def shift(value, far, near, step):
    pairs = [(f * near + n, ((f + step) % far) * near + n) for f in range(far) for n in range(near)]
    return lax.ppermute(value, "seq", pairs)


def finish(total, k_gain):
    key_head = total[:, :HEAD_SIZE]
    inverse = lax.rsqrt(jnp.mean(key_head * key_head, axis=-1, keepdims=True) + 1e-05)
    key_head = (key_head * inverse * k_gain).astype(jnp.bfloat16)
    return jnp.concatenate([key_head, total[:, HEAD_SIZE:].astype(jnp.bfloat16)], axis=1)


def per_device(
    seq_size,
    queries,
    image_token_rows,
    key_matrix,
    value_matrix,
    k_gain,
    image_counts,
    image_lo,
    image_hi,
    gate,
):
    img_rows, model_width = image_token_rows.shape
    local_heads = key_matrix.shape[1] // HEAD_SIZE
    flags = text_flags(image_lo, image_hi)
    gate_row = jnp.broadcast_to(gate[:, None], (1, HEAD_SIZE))
    group = lax.axis_index("group")
    core = lax.axis_index("head")
    index = lax.axis_index("seq")

    def head_weights(head):
        at = slice(head * HEAD_SIZE, (head + 1) * HEAD_SIZE)
        return jnp.concatenate([key_matrix[:, at], value_matrix[:, at]], axis=1)

    out = None
    if (seq_size, local_heads) != (8, 2) or img_rows % 32 or lax.axis_size("group") != 2:
        info = jnp.concatenate([image_counts, jnp.zeros((1,), jnp.int32)])
        for head in range(local_heads):
            weights = lax.all_gather(head_weights(head), "seq", axis=0, tiled=True)
            total = jnp.dot(image_token_rows, weights, preferred_element_type=jnp.float32)
            kv = lax.all_gather(finish(total, k_gain), "seq", axis=0, tiled=True)
            out = attend(queries, flags, gate_row, [kv], info, head, out)
        return out

    near = 2
    far = seq_size // near
    mine_far, mine_near = index // near, index % near
    shards = jnp.stack(
        [((mine_far - k) % far) * near + (mine_near ^ b) for k in range(far) for b in range(near)]
    ).astype(jnp.int32)
    width = model_width // seq_size // 2
    across = [(0, 1), (1, 0)]
    half = lax.dynamic_slice_in_dim(shards, core * (seq_size // 2), seq_size // 2)
    block = pick_blocks(2 * half + (1 - group), image_token_rows, width)
    direct = lax.ppermute(block, "group", across)
    parts = [
        lax.dynamic_slice_in_dim(head_weights(head), group * width, width)
        for head in range(local_heads)
    ]
    size = seq_size
    w0, w1 = parts
    a1, a3 = shift(w0, far, near, 1), shift(w0, far, near, 3)
    a0x, b0x = swap(w0, size), swap(w1, size)
    a2 = shift(after(a1, a3), far, near, 1)
    a1x = swap(after(a1, a3), size)
    a3x = swap(after(a3, a0x, b0x), size)
    b1 = shift(after(w1, a3, a0x, b0x), far, near, 1)
    mine = pick_blocks(
        after(2 * shards + group, a1, a3, a0x, b0x), image_token_rows, width
    )
    a2x = swap(after(a2, mine), size)
    b3 = shift(after(w1, a1x), far, near, 3)
    b2 = shift(b1, far, near, 1)
    b1x = shift(after(b0x, a3x), far, near, 1)
    b3x = swap(b3, size)
    passed = lax.ppermute(after(direct, a1x, a3x, a2x, b1, b3), "head", across)
    b2x = swap(b2, size)
    spreads = [[w0, a0x, a1, a1x, a2, a2x, a3, a3x], [w1, b0x, b1, b1x, b2, b2x, b3, b3x]]
    core_arg = core.reshape(1).astype(jnp.int32)
    other0, own0 = project(core_arg, mine, direct, passed, spreads[0])
    k0 = finish(own0 + lax.ppermute(other0, "group", across), k_gain)
    other1, own1 = project(core_arg, mine, direct, passed, after(spreads[1], k0))
    a1, a3, a0x = shift(k0, far, near, 1), shift(k0, far, near, 3), swap(k0, size)
    k1 = finish(own1 + after(lax.ppermute(other1, "group", across), a0x), k_gain)

    def part(head, slots, pieces, previous=None, state=None, last=True):
        here = jnp.concatenate([image_counts, jnp.stack([shards[j] for j in slots])])
        return attend(queries, flags, gate_row, pieces, here, head, previous, state, last)

    a2 = shift(a1, far, near, 1)
    a1x, a3x = swap(a1, size), swap(a3, size)
    b0x = swap(k1, size)
    b1 = shift(after(k1, a1, a3), far, near, 1)
    b3 = shift(after(k1, a1, a3), far, near, 3)
    state = part(0, (0, 1, 2, 6), [k0, a0x, a1, a3], last=False)
    a2x = swap(a2, size)
    b2 = shift(b1, far, near, 1)
    b1x = shift(after(b0x, a3x), far, near, 1)
    b3x = swap(b3, size)
    b2x = swap(after(b2, state), size)
    out = part(0, (3, 7, 4, 5), [a1x, a3x, a2, a2x], state=state)
    state = part(1, (0, 1, 2, 6), [k1, b0x, b1, b3], last=False)
    return part(1, (3, 7, 4, 5), [b1x, b3x, b2, b2x], out, state)


def solution(mesh):
    in_specs = (
        P(("group", "seq"), "head"),
        P(("group", "seq"), None),
        P("seq", "head"),
        P("seq", "head"),
        P(),
        P("group"),
        P(("group", "seq")),
        P(("group", "seq")),
        P(),
    )
    out_specs = P(("group", "seq"), "head")
    return jax.shard_map(
        functools.partial(per_device, mesh.shape["seq"]),
        mesh=mesh,
        in_specs=in_specs,
        out_specs=out_specs,
        check_vma=False,
    )
```

```python
import functools
import math

import jax
import jax.numpy as jnp
from jax import lax
from jax.experimental import pallas as pl
from jax.experimental.pallas import tpu as pltpu
from jax.sharding import PartitionSpec as P

HEAD_SIZE = 128
QUERY_GROUP = 8
SLOT = 1664
NIMG = 2
CHUNK = 256
HEADS_AT_ONCE = 4
BIG = 2.0**98


def attention_kernel(slots, piece, arrays, resumed, last, info, q_ref, flag_ref, gate_ref, *refs):
    o_ref, keys, vals, *buffers = refs[-5:]
    state_ref = refs[arrays] if resumed else None
    rows = slots * piece

    @pl.when(pl.program_id(0) == 0)
    def _():
        lane = lax.broadcasted_iota(jnp.int32, (piece, HEAD_SIZE), 1)
        row = lax.broadcasted_iota(jnp.int32, (piece, HEAD_SIZE), 0)
        ones = jnp.ones((piece, HEAD_SIZE), jnp.bfloat16)
        for j, kv in enumerate(pieces_of(refs[:arrays], piece)):
            at = slice(j * piece, (j + 1) * piece)
            position = row + info[NIMG + j] * piece
            flags = jnp.zeros((piece, HEAD_SIZE), jnp.float32)
            for i in range(NIMG):
                mine = (position >= i * SLOT) & (position < (i + 1) * SLOT)
                beyond = mine & (position - i * SLOT >= info[i])
                hit = (mine & (lane == i)) | (beyond & (lane == NIMG))
                flags = jnp.where(hit, -BIG, flags)
            keys[at, :HEAD_SIZE] = kv[:, :HEAD_SIZE]
            keys[at, HEAD_SIZE:] = flags.astype(jnp.bfloat16)
            vals[at, :HEAD_SIZE] = kv[:, HEAD_SIZE:]
            vals[at, HEAD_SIZE:] = ones

    def columns_of(g, first, count):
        at = (3 * (pl.program_id(0) * HEADS_AT_ONCE + g) + first) * HEAD_SIZE
        return pl.ds(pl.multiple_of(at, HEAD_SIZE), count * HEAD_SIZE)

    def across(tile, chunk):
        return jnp.concatenate([tile] * ((chunk.stop - chunk.start) // HEAD_SIZE), axis=1)

    scale = math.log2(math.e) / math.sqrt(HEAD_SIZE)
    gain = jnp.tanh(gate_ref[...])
    rows_q = q_ref.shape[0]
    pairs = HEADS_AT_ONCE // 2
    top = None
    for i in range(pairs + 1):
        now, later = buffers[(i + 1) % 2], buffers[i % 2]
        highest = total = None
        if i < pairs:
            wide = jnp.concatenate(
                [
                    jnp.concatenate(
                        [q_ref[:, g * HEAD_SIZE : (g + 1) * HEAD_SIZE], flag_ref[...]], axis=1
                    )
                    for g in (2 * i, 2 * i + 1)
                ],
                axis=0,
            )
        for start in range(0, rows, CHUNK):
            chunk = slice(start, min(start + CHUNK, rows))
            if i < pairs:
                part = lax.dot_general(
                    wide,
                    keys[chunk, :],
                    (((1,), (1,)), ((), ())),
                    preferred_element_type=jnp.float32,
                )
                later[:, chunk] = part
                for lane in range(0, part.shape[1], HEAD_SIZE):
                    best = part[:, lane : lane + HEAD_SIZE]
                    highest = best if highest is None else jnp.maximum(highest, best)
            if i > 0:
                weights = jnp.exp2((now[:, chunk] - across(top, chunk)) * scale).astype(jnp.bfloat16)
                term = jnp.dot(weights, vals[chunk, :], preferred_element_type=jnp.float32)
                total = term if total is None else total + term
        if i > 0:
            for half in range(2):
                g = 2 * (i - 1) + half
                mine = slice(half * rows_q, (half + 1) * rows_q)
                whole, peak = total[mine], top[mine]
                if resumed:
                    before = state_ref[:, columns_of(g, 0, 2)]
                    fade = jnp.exp2((before_top[half] - peak) * scale)
                    whole = whole + before * jnp.concatenate([fade, fade], axis=1)
                if last:
                    at = slice(g * HEAD_SIZE, (g + 1) * HEAD_SIZE)
                    out = gain * (whole[:, :HEAD_SIZE] / whole[:, HEAD_SIZE:])
                    o_ref[:, at] = out.astype(o_ref.dtype)
                else:
                    o_ref[:, columns_of(g, 0, 2)] = whole
                    o_ref[:, columns_of(g, 2, 1)] = peak
        if i < pairs:
            top = jnp.broadcast_to(jnp.max(highest, axis=1, keepdims=True), highest.shape)
            if resumed:
                before_top = [state_ref[:, columns_of(g, 2, 1)] for g in (2 * i, 2 * i + 1)]
                top = jnp.maximum(top, jnp.concatenate(before_top, axis=0))


def attend(queries, flags, gate_row, pieces, info, head, previous, state=None, last=True):
    text_rows, width = queries.shape
    piece = pieces[0].shape[0]
    rows = sum(held.shape[0] for held in pieces)
    slots = rows // piece
    steps = QUERY_GROUP // HEADS_AT_ONCE
    block = HEADS_AT_ONCE * HEAD_SIZE
    state_spec = in_vmem(1)[0]
    if last:
        out_spec = pl.BlockSpec((text_rows, block), lambda g, s: (0, head * steps + g))
        out_shape = jax.ShapeDtypeStruct((text_rows, width), jnp.bfloat16)
    else:
        out_spec = state_spec
        out_shape = jax.ShapeDtypeStruct((text_rows, 3 * QUERY_GROUP * HEAD_SIZE), jnp.float32)
    in_specs = [
        pl.BlockSpec((text_rows, block), lambda g, s: (0, head * steps + g)),
        pl.BlockSpec((text_rows, HEAD_SIZE), lambda g, s: (0, 0)),
        pl.BlockSpec((1, HEAD_SIZE), lambda g, s: (0, 0)),
    ] + in_vmem(len(pieces))
    args = [info, queries, flags, gate_row, *pieces]
    if state is not None:
        in_specs.append(state_spec)
        args.append(state)
    aliases = {}
    if previous is not None:
        in_specs.append(pl.BlockSpec(memory_space=pl.ANY))
        aliases = {len(args): 0}
        args.append(previous)
    return pl.pallas_call(
        functools.partial(
            attention_kernel, slots, piece, len(pieces), state is not None, last
        ),
        out_shape=out_shape,
        grid_spec=pltpu.PrefetchScalarGridSpec(
            num_scalar_prefetch=1,
            grid=(steps,),
            in_specs=in_specs,
            out_specs=out_spec,
            scratch_shapes=[
                pltpu.VMEM((rows, 2 * HEAD_SIZE), jnp.bfloat16),
                pltpu.VMEM((rows, 2 * HEAD_SIZE), jnp.bfloat16),
                pltpu.VMEM((2 * text_rows, rows), jnp.float32),
                pltpu.VMEM((2 * text_rows, rows), jnp.float32),
            ],
        ),
        input_output_aliases=aliases,
        compiler_params=pltpu.CompilerParams(vmem_limit_bytes=28 * 2**20),
        cost_estimate=pl.CostEstimate(
            flops=8 * QUERY_GROUP * text_rows * rows * HEAD_SIZE,
            bytes_accessed=2 * rows * 2 * HEAD_SIZE,
            transcendentals=QUERY_GROUP * text_rows * rows,
        ),
    )(*args)


def text_flags(image_lo, image_hi):
    lane = jnp.arange(HEAD_SIZE)[None, :]
    hidden = (lane < NIMG) & ((lane < image_lo[:, None]) | (lane >= image_hi[:, None]))
    return (hidden | (lane == NIMG)).astype(jnp.bfloat16)


def pick_blocks(which, image, width):
    rows = image.shape[0]
    count = which.shape[0]

    def kernel(which_ref, image_ref, o_ref, sems):
        copies = []
        for j in range(count):
            column = pl.multiple_of(which_ref[j] * width, width)
            copies.append(
                pltpu.make_async_copy(image_ref.at[:, pl.ds(column, width)], o_ref.at[j], sems.at[j])
            )
        for copy in copies:
            copy.start()
        for copy in copies:
            copy.wait()

    return pl.pallas_call(
        kernel,
        out_shape=jax.ShapeDtypeStruct((count, rows, width), image.dtype),
        grid_spec=pltpu.PrefetchScalarGridSpec(
            num_scalar_prefetch=1,
            grid=(),
            in_specs=[pl.BlockSpec(memory_space=pl.ANY)],
            out_specs=pl.BlockSpec(memory_space=pltpu.VMEM),
            scratch_shapes=[pltpu.SemaphoreType.DMA((count,))],
        ),
        compiler_params=pltpu.CompilerParams(vmem_limit_bytes=8 * 2**20),
        cost_estimate=pl.CostEstimate(
            flops=0, bytes_accessed=4 * count * rows * width, transcendentals=0
        ),
    )(which, image)


def in_vmem(count):
    return [pl.BlockSpec(memory_space=pltpu.VMEM)] * count


def pieces_of(refs, rows):
    return [ref[i : i + rows, :] for ref in refs for i in range(0, ref.shape[0], rows)]


def dots(blocks, weights):
    total = None
    for block, weight in zip(blocks, weights):
        term = jnp.dot(block, weight, preferred_element_type=jnp.float32)
        total = term if total is None else total + term
    return total


def project(core, mine, direct, passed, weights, order):
    count, rows, width = mine.shape
    columns = weights[0].shape[1]
    arrays = len(weights)

    def kernel(core_ref, mine_ref, direct_ref, passed_ref, *refs):
        other_ref, own_ref = refs[-2:]
        given = pieces_of(refs[:arrays], width)
        held = [given[order.index(j)] for j in range(count)]

        def run(*halves):
            blocks = [half[j] for half in halves for j in range(count // 2)]
            other_ref[...] = dots(blocks, held)

        @pl.when(core_ref[0] == 0)
        def _():
            run(direct_ref, passed_ref)

        @pl.when(core_ref[0] != 0)
        def _():
            run(passed_ref, direct_ref)

        own_ref[...] = dots([mine_ref[j] for j in range(count)], held)

    shape = jax.ShapeDtypeStruct((rows, columns), jnp.float32)
    return pl.pallas_call(
        kernel,
        out_shape=(shape, shape),
        in_specs=[pl.BlockSpec(memory_space=pltpu.SMEM)] + in_vmem(3 + arrays),
        out_specs=tuple(in_vmem(2)),
        compiler_params=pltpu.CompilerParams(vmem_limit_bytes=16 * 2**20),
        cost_estimate=pl.CostEstimate(
            flops=4 * count * rows * width * columns,
            bytes_accessed=4 * count * width * (rows + columns),
            transcendentals=0,
        ),
    )(core, mine, direct, passed, *weights)


def after(value, *others):
    return lax.optimization_barrier((value, *others))[0]


def swap(value, size):
    return lax.ppermute(value, "seq", [(i, i ^ 1) for i in range(size)])


def shift(value, far, near, step):
    pairs = [(f * near + n, ((f + step) % far) * near + n) for f in range(far) for n in range(near)]
    return lax.ppermute(value, "seq", pairs)


def finish(total, k_gain):
    key_head = total[:, :HEAD_SIZE]
    inverse = lax.rsqrt(jnp.mean(key_head * key_head, axis=-1, keepdims=True) + 1e-05)
    key_head = (key_head * inverse * k_gain).astype(jnp.bfloat16)
    return jnp.concatenate([key_head, total[:, HEAD_SIZE:].astype(jnp.bfloat16)], axis=1)


def per_device(
    seq_size,
    queries,
    image_token_rows,
    key_matrix,
    value_matrix,
    k_gain,
    image_counts,
    image_lo,
    image_hi,
    gate,
):
    img_rows, model_width = image_token_rows.shape
    local_heads = key_matrix.shape[1] // HEAD_SIZE
    flags = text_flags(image_lo, image_hi)
    gate_row = jnp.broadcast_to(gate[:, None], (1, HEAD_SIZE))
    group = lax.axis_index("group")
    core = lax.axis_index("head")
    index = lax.axis_index("seq")

    def head_weights(head):
        at = slice(head * HEAD_SIZE, (head + 1) * HEAD_SIZE)
        return jnp.concatenate([key_matrix[:, at], value_matrix[:, at]], axis=1)

    out = None
    if (seq_size, local_heads) != (8, 2) or img_rows % 32 or lax.axis_size("group") != 2:
        info = jnp.concatenate([image_counts, jnp.zeros((1,), jnp.int32)])
        for head in range(local_heads):
            weights = lax.all_gather(head_weights(head), "seq", axis=0, tiled=True)
            total = jnp.dot(image_token_rows, weights, preferred_element_type=jnp.float32)
            kv = lax.all_gather(finish(total, k_gain), "seq", axis=0, tiled=True)
            out = attend(queries, flags, gate_row, [kv], info, head, out)
        return out

    near = 2
    far = seq_size // near
    mine_far, mine_near = index // near, index % near
    shards = jnp.stack(
        [((mine_far - k) % far) * near + (mine_near ^ b) for k in range(far) for b in range(near)]
    ).astype(jnp.int32)
    width = model_width // seq_size // 2
    across = [(0, 1), (1, 0)]
    half = lax.dynamic_slice_in_dim(shards, core * (seq_size // 2), seq_size // 2)
    block = pick_blocks(2 * half + (1 - group), image_token_rows, width)
    direct = lax.ppermute(block, "group", across)
    parts = [
        lax.dynamic_slice_in_dim(head_weights(head), group * width, width)
        for head in range(local_heads)
    ]
    size = seq_size
    w0, w1 = parts
    a1, a3 = shift(w0, far, near, 1), shift(w0, far, near, 3)
    a0x, b0x = swap(w0, size), swap(w1, size)
    a2 = shift(after(a1, a3), far, near, 1)
    a1x = swap(after(a1, a3), size)
    a3x = swap(after(a3, a0x, b0x), size)
    b1 = shift(after(w1, a3, a0x, b0x), far, near, 1)
    mine = pick_blocks(
        after(2 * shards + group, a1, a3, a0x, b0x), image_token_rows, width
    )
    a2x = swap(after(a2, mine), size)
    b3 = shift(after(w1, a1x), far, near, 3)
    b2 = shift(b1, far, near, 1)
    b1x = shift(after(b0x, a3x), far, near, 1)
    b3x = swap(b3, size)
    passed = lax.ppermute(after(direct, a1x, a3x, a2x, b1, b3), "head", across)
    b2x = swap(b2, size)
    spreads = [[w0, a0x, a1, a1x, a2, a2x, a3, a3x], [w1, b0x, b1, b1x, b2, b2x, b3, b3x]]
    core_arg = core.reshape(1).astype(jnp.int32)
    other0, own0 = project(
        core_arg, mine, direct, passed, spreads[0], tuple(range(seq_size))
    )
    k0 = finish(own0 + lax.ppermute(other0, "group", across), k_gain)
    other1, own1 = project(
        core_arg, mine, direct, passed, after(spreads[1], k0), tuple(range(seq_size))
    )
    a1, a3, a0x = shift(k0, far, near, 1), shift(k0, far, near, 3), swap(k0, size)
    k1 = finish(own1 + after(lax.ppermute(other1, "group", across), a0x), k_gain)

    def part(head, slots, pieces, previous=None, state=None, last=True):
        here = jnp.concatenate([image_counts, jnp.stack([shards[j] for j in slots])])
        return attend(queries, flags, gate_row, pieces, here, head, previous, state, last)

    a2 = shift(a1, far, near, 1)
    ax = swap(jnp.concatenate([a1, a3]), size)
    b0x = swap(k1, size)
    b1 = shift(after(k1, a1, a3), far, near, 1)
    b3 = shift(after(k1, a1, a3), far, near, 3)
    state = part(0, (0, 1, 2, 6), [k0, a0x, a1, a3], last=False)
    a2x = swap(after(a2, state), size)
    bx = shift(jnp.concatenate([b0x, b1]), far, near, 1)
    b3x = swap(b3, size)
    b2x = swap(bx[img_rows:], size)
    out = part(0, (4, 5, 3, 7), [a2, a2x, ax], state=state)
    state = part(1, (0, 1, 2, 6), [k1, b0x, b1, b3], last=False)
    return part(1, (5, 3, 4, 7), [b2x, bx, b3x], out, state)


def solution(mesh):
    in_specs = (
        P(("group", "seq"), "head"),
        P(("group", "seq"), None),
        P("seq", "head"),
        P("seq", "head"),
        P(),
        P("group"),
        P(("group", "seq")),
        P(("group", "seq")),
        P(),
    )
    out_specs = P(("group", "seq"), "head")
    return jax.shard_map(
        functools.partial(per_device, mesh.shape["seq"]),
        mesh=mesh,
        in_specs=in_specs,
        out_specs=out_specs,
        check_vma=False,
    )
```

```python
import functools
import math

import jax
import jax.numpy as jnp
from jax import lax
from jax.experimental import pallas as pl
from jax.experimental.pallas import tpu as pltpu
from jax.sharding import PartitionSpec as P

HEAD_SIZE = 128
QUERY_GROUP = 8
SLOT = 1664
NIMG = 2
CHUNK = 256
HEADS_AT_ONCE = 4
BIG = 2.0**98


def attention_kernel(slots, piece, arrays, resumed, last, info, q_ref, flag_ref, gate_ref, *refs):
    o_ref, keys, vals, *buffers = refs[-5:]
    state_ref = refs[arrays] if resumed else None
    rows = slots * piece

    @pl.when(pl.program_id(0) == 0)
    def _():
        lane = lax.broadcasted_iota(jnp.int32, (piece, HEAD_SIZE), 1)
        row = lax.broadcasted_iota(jnp.int32, (piece, HEAD_SIZE), 0)
        ones = jnp.ones((piece, HEAD_SIZE), jnp.bfloat16)
        for j, kv in enumerate(pieces_of(refs[:arrays], piece)):
            at = slice(j * piece, (j + 1) * piece)
            position = row + info[NIMG + j] * piece
            flags = jnp.zeros((piece, HEAD_SIZE), jnp.float32)
            for i in range(NIMG):
                mine = (position >= i * SLOT) & (position < (i + 1) * SLOT)
                beyond = mine & (position - i * SLOT >= info[i])
                hit = (mine & (lane == i)) | (beyond & (lane == NIMG))
                flags = jnp.where(hit, -BIG, flags)
            keys[at, :HEAD_SIZE] = kv[:, :HEAD_SIZE]
            keys[at, HEAD_SIZE:] = flags.astype(jnp.bfloat16)
            vals[at, :HEAD_SIZE] = kv[:, HEAD_SIZE:]
            vals[at, HEAD_SIZE:] = ones

    def columns_of(g, first, count):
        at = (3 * (pl.program_id(0) * HEADS_AT_ONCE + g) + first) * HEAD_SIZE
        return pl.ds(pl.multiple_of(at, HEAD_SIZE), count * HEAD_SIZE)

    def across(tile, chunk):
        return jnp.concatenate([tile] * ((chunk.stop - chunk.start) // HEAD_SIZE), axis=1)

    scale = math.log2(math.e) / math.sqrt(HEAD_SIZE)
    gain = jnp.tanh(gate_ref[...])
    rows_q = q_ref.shape[0]
    pairs = HEADS_AT_ONCE // 2
    top = None
    for i in range(pairs + 1):
        now, later = buffers[(i + 1) % 2], buffers[i % 2]
        highest = total = None
        if i < pairs:
            wide = jnp.concatenate(
                [
                    jnp.concatenate(
                        [q_ref[:, g * HEAD_SIZE : (g + 1) * HEAD_SIZE], flag_ref[...]], axis=1
                    )
                    for g in (2 * i, 2 * i + 1)
                ],
                axis=0,
            )
        for start in range(0, rows, CHUNK):
            chunk = slice(start, min(start + CHUNK, rows))
            if i < pairs:
                part = lax.dot_general(
                    wide,
                    keys[chunk, :],
                    (((1,), (1,)), ((), ())),
                    preferred_element_type=jnp.float32,
                )
                later[:, chunk] = part
                for lane in range(0, part.shape[1], HEAD_SIZE):
                    best = part[:, lane : lane + HEAD_SIZE]
                    highest = best if highest is None else jnp.maximum(highest, best)
            if i > 0:
                weights = jnp.exp2((now[:, chunk] - across(top, chunk)) * scale).astype(jnp.bfloat16)
                term = jnp.dot(weights, vals[chunk, :], preferred_element_type=jnp.float32)
                total = term if total is None else total + term
        if i > 0:
            for half in range(2):
                g = 2 * (i - 1) + half
                mine = slice(half * rows_q, (half + 1) * rows_q)
                whole, peak = total[mine], top[mine]
                if resumed:
                    before = state_ref[:, columns_of(g, 0, 2)]
                    fade = jnp.exp2((before_top[half] - peak) * scale)
                    whole = whole + before * jnp.concatenate([fade, fade], axis=1)
                if last:
                    at = slice(g * HEAD_SIZE, (g + 1) * HEAD_SIZE)
                    out = gain * (whole[:, :HEAD_SIZE] / whole[:, HEAD_SIZE:])
                    o_ref[:, at] = out.astype(o_ref.dtype)
                else:
                    o_ref[:, columns_of(g, 0, 2)] = whole
                    o_ref[:, columns_of(g, 2, 1)] = peak
        if i < pairs:
            top = jnp.broadcast_to(jnp.max(highest, axis=1, keepdims=True), highest.shape)
            if resumed:
                before_top = [state_ref[:, columns_of(g, 2, 1)] for g in (2 * i, 2 * i + 1)]
                top = jnp.maximum(top, jnp.concatenate(before_top, axis=0))


def attend(queries, flags, gate_row, pieces, info, head, previous, state=None, last=True):
    text_rows, width = queries.shape
    piece = pieces[0].shape[0]
    rows = sum(held.shape[0] for held in pieces)
    slots = rows // piece
    steps = QUERY_GROUP // HEADS_AT_ONCE
    block = HEADS_AT_ONCE * HEAD_SIZE
    state_spec = in_vmem(1)[0]
    if last:
        out_spec = pl.BlockSpec((text_rows, block), lambda g, s: (0, head * steps + g))
        out_shape = jax.ShapeDtypeStruct((text_rows, width), jnp.bfloat16)
    else:
        out_spec = state_spec
        out_shape = jax.ShapeDtypeStruct((text_rows, 3 * QUERY_GROUP * HEAD_SIZE), jnp.float32)
    in_specs = [
        pl.BlockSpec((text_rows, block), lambda g, s: (0, head * steps + g)),
        pl.BlockSpec((text_rows, HEAD_SIZE), lambda g, s: (0, 0)),
        pl.BlockSpec((1, HEAD_SIZE), lambda g, s: (0, 0)),
    ] + in_vmem(len(pieces))
    args = [info, queries, flags, gate_row, *pieces]
    if state is not None:
        in_specs.append(state_spec)
        args.append(state)
    aliases = {}
    if previous is not None:
        in_specs.append(pl.BlockSpec(memory_space=pl.ANY))
        aliases = {len(args): 0}
        args.append(previous)
    return pl.pallas_call(
        functools.partial(
            attention_kernel, slots, piece, len(pieces), state is not None, last
        ),
        out_shape=out_shape,
        grid_spec=pltpu.PrefetchScalarGridSpec(
            num_scalar_prefetch=1,
            grid=(steps,),
            in_specs=in_specs,
            out_specs=out_spec,
            scratch_shapes=[
                pltpu.VMEM((rows, 2 * HEAD_SIZE), jnp.bfloat16),
                pltpu.VMEM((rows, 2 * HEAD_SIZE), jnp.bfloat16),
                pltpu.VMEM((2 * text_rows, rows), jnp.float32),
                pltpu.VMEM((2 * text_rows, rows), jnp.float32),
            ],
        ),
        input_output_aliases=aliases,
        compiler_params=pltpu.CompilerParams(vmem_limit_bytes=28 * 2**20),
        cost_estimate=pl.CostEstimate(
            flops=8 * QUERY_GROUP * text_rows * rows * HEAD_SIZE,
            bytes_accessed=2 * rows * 2 * HEAD_SIZE,
            transcendentals=QUERY_GROUP * text_rows * rows,
        ),
    )(*args)


def text_flags(image_lo, image_hi):
    lane = jnp.arange(HEAD_SIZE)[None, :]
    hidden = (lane < NIMG) & ((lane < image_lo[:, None]) | (lane >= image_hi[:, None]))
    return (hidden | (lane == NIMG)).astype(jnp.bfloat16)


def pick_blocks(which, image, width):
    rows = image.shape[0]
    count = which.shape[0]

    def kernel(which_ref, image_ref, o_ref, sems):
        copies = []
        for j in range(count):
            column = pl.multiple_of(which_ref[j] * width, width)
            copies.append(
                pltpu.make_async_copy(image_ref.at[:, pl.ds(column, width)], o_ref.at[j], sems.at[j])
            )
        for copy in copies:
            copy.start()
        for copy in copies:
            copy.wait()

    return pl.pallas_call(
        kernel,
        out_shape=jax.ShapeDtypeStruct((count, rows, width), image.dtype),
        grid_spec=pltpu.PrefetchScalarGridSpec(
            num_scalar_prefetch=1,
            grid=(),
            in_specs=[pl.BlockSpec(memory_space=pl.ANY)],
            out_specs=pl.BlockSpec(memory_space=pltpu.VMEM),
            scratch_shapes=[pltpu.SemaphoreType.DMA((count,))],
        ),
        compiler_params=pltpu.CompilerParams(vmem_limit_bytes=8 * 2**20),
        cost_estimate=pl.CostEstimate(
            flops=0, bytes_accessed=4 * count * rows * width, transcendentals=0
        ),
    )(which, image)


def in_vmem(count):
    return [pl.BlockSpec(memory_space=pltpu.VMEM)] * count


def pieces_of(refs, rows):
    return [ref[i : i + rows, :] for ref in refs for i in range(0, ref.shape[0], rows)]


def dots(blocks, weights):
    total = None
    for block, weight in zip(blocks, weights):
        term = jnp.dot(block, weight, preferred_element_type=jnp.float32)
        total = term if total is None else total + term
    return total


def project(core, mine, direct, passed, weights, order):
    count, rows, width = mine.shape
    columns = weights[0].shape[1]
    arrays = len(weights)

    def kernel(core_ref, mine_ref, direct_ref, passed_ref, *refs):
        other_ref, own_ref = refs[-2:]
        given = pieces_of(refs[:arrays], width)
        held = [given[order.index(j)] for j in range(count)]

        def run(*halves):
            blocks = [half[j] for half in halves for j in range(count // 2)]
            other_ref[...] = dots(blocks, held)

        @pl.when(core_ref[0] == 0)
        def _():
            run(direct_ref, passed_ref)

        @pl.when(core_ref[0] != 0)
        def _():
            run(passed_ref, direct_ref)

        own_ref[...] = dots([mine_ref[j] for j in range(count)], held)

    shape = jax.ShapeDtypeStruct((rows, columns), jnp.float32)
    return pl.pallas_call(
        kernel,
        out_shape=(shape, shape),
        in_specs=[pl.BlockSpec(memory_space=pltpu.SMEM)] + in_vmem(3 + arrays),
        out_specs=tuple(in_vmem(2)),
        compiler_params=pltpu.CompilerParams(vmem_limit_bytes=16 * 2**20),
        cost_estimate=pl.CostEstimate(
            flops=4 * count * rows * width * columns,
            bytes_accessed=4 * count * width * (rows + columns),
            transcendentals=0,
        ),
    )(core, mine, direct, passed, *weights)


def after(value, *others):
    return lax.optimization_barrier((value, *others))[0]


def swap(value, size):
    return lax.ppermute(value, "seq", [(i, i ^ 1) for i in range(size)])


def shift(value, far, near, step):
    pairs = [(f * near + n, ((f + step) % far) * near + n) for f in range(far) for n in range(near)]
    return lax.ppermute(value, "seq", pairs)


def finish(total, k_gain):
    key_head = total[:, :HEAD_SIZE]
    inverse = lax.rsqrt(jnp.mean(key_head * key_head, axis=-1, keepdims=True) + 1e-05)
    key_head = (key_head * inverse * k_gain).astype(jnp.bfloat16)
    return jnp.concatenate([key_head, total[:, HEAD_SIZE:].astype(jnp.bfloat16)], axis=1)


def per_device(
    seq_size,
    queries,
    image_token_rows,
    key_matrix,
    value_matrix,
    k_gain,
    image_counts,
    image_lo,
    image_hi,
    gate,
):
    img_rows, model_width = image_token_rows.shape
    local_heads = key_matrix.shape[1] // HEAD_SIZE
    flags = text_flags(image_lo, image_hi)
    gate_row = jnp.broadcast_to(gate[:, None], (1, HEAD_SIZE))
    group = lax.axis_index("group")
    core = lax.axis_index("head")
    index = lax.axis_index("seq")

    def head_weights(head):
        at = slice(head * HEAD_SIZE, (head + 1) * HEAD_SIZE)
        return jnp.concatenate([key_matrix[:, at], value_matrix[:, at]], axis=1)

    out = None
    if (seq_size, local_heads) != (8, 2) or img_rows % 32 or lax.axis_size("group") != 2:
        info = jnp.concatenate([image_counts, jnp.zeros((1,), jnp.int32)])
        for head in range(local_heads):
            weights = lax.all_gather(head_weights(head), "seq", axis=0, tiled=True)
            total = jnp.dot(image_token_rows, weights, preferred_element_type=jnp.float32)
            kv = lax.all_gather(finish(total, k_gain), "seq", axis=0, tiled=True)
            out = attend(queries, flags, gate_row, [kv], info, head, out)
        return out

    near = 2
    far = seq_size // near
    mine_far, mine_near = index // near, index % near
    shards = jnp.stack(
        [((mine_far - k) % far) * near + (mine_near ^ b) for k in range(far) for b in range(near)]
    ).astype(jnp.int32)
    width = model_width // seq_size // 2
    across = [(0, 1), (1, 0)]
    half = lax.dynamic_slice_in_dim(shards, core * (seq_size // 2), seq_size // 2)
    block = pick_blocks(2 * half + (1 - group), image_token_rows, width)
    direct = lax.ppermute(block, "group", across)
    parts = [
        lax.dynamic_slice_in_dim(head_weights(head), group * width, width)
        for head in range(local_heads)
    ]
    size = seq_size
    w0, w1 = parts
    a1, a3 = shift(w0, far, near, 1), shift(w0, far, near, 3)
    a0x, b0x = swap(w0, size), swap(w1, size)
    a2 = shift(after(a1, a3), far, near, 1)
    a1x = swap(after(a1, a3), size)
    a3x = swap(after(a3, a0x, b0x), size)
    b1 = shift(after(w1, a3, a0x, b0x), far, near, 1)
    mine = pick_blocks(
        after(2 * shards + group, a1, a3, a0x, b0x), image_token_rows, width
    )
    a2x = swap(after(a2, mine), size)
    b3 = shift(after(w1, a1x), far, near, 3)
    b2 = shift(b1, far, near, 1)
    b1x = shift(after(b0x, a3x), far, near, 1)
    b3x = swap(b3, size)
    passed = lax.ppermute(after(direct, a1x, a3x, a2x, b1, b3), "head", across)
    b2x = swap(b2, size)
    spreads = [[w0, a0x, a1, a1x, a2, a2x, a3, a3x], [w1, b0x, b1, b1x, b2, b2x, b3, b3x]]
    core_arg = core.reshape(1).astype(jnp.int32)
    other0, own0 = project(
        core_arg, mine, direct, passed, spreads[0], tuple(range(seq_size))
    )
    k0 = finish(own0 + lax.ppermute(other0, "group", across), k_gain)
    other1, own1 = project(
        core_arg, mine, direct, passed, after(spreads[1], k0), tuple(range(seq_size))
    )
    a1, a3, a0x = shift(k0, far, near, 1), shift(k0, far, near, 3), swap(k0, size)
    k1 = finish(own1 + after(lax.ppermute(other1, "group", across), a0x), k_gain)

    def part(head, slots, pieces, previous=None, state=None, last=True):
        here = jnp.concatenate([image_counts, jnp.stack([shards[j] for j in slots])])
        return attend(queries, flags, gate_row, pieces, here, head, previous, state, last)

    a2 = shift(a1, far, near, 1)
    ax = swap(jnp.concatenate([a1, a3]), size)
    b0x = swap(k1, size)
    b1 = shift(k1, far, near, 1)
    b3 = shift(k1, far, near, 3)
    state = part(0, (0, 1, 2, 6), [k0, a0x, a1, a3], last=False)
    a2x = swap(after(a2, state), size)
    bx = shift(jnp.concatenate([b0x, b1]), far, near, 1)
    b3x = swap(b3, size)
    b2x = swap(bx[img_rows:], size)
    out = part(0, (4, 5, 3, 7), [a2, a2x, ax], state=state)
    state = part(1, (0, 1, 2, 6), [k1, b0x, b1, b3], last=False)
    return part(1, (5, 3, 4, 7), [b2x, bx, b3x], out, state)


def solution(mesh):
    in_specs = (
        P(("group", "seq"), "head"),
        P(("group", "seq"), None),
        P("seq", "head"),
        P("seq", "head"),
        P(),
        P("group"),
        P(("group", "seq")),
        P(("group", "seq")),
        P(),
    )
    out_specs = P(("group", "seq"), "head")
    return jax.shard_map(
        functools.partial(per_device, mesh.shape["seq"]),
        mesh=mesh,
        in_specs=in_specs,
        out_specs=out_specs,
        check_vma=False,
    )
```

```python
import functools
import math

import jax
import jax.numpy as jnp
from jax import lax
from jax.experimental import pallas as pl
from jax.experimental.pallas import tpu as pltpu
from jax.sharding import PartitionSpec as P

HEAD_SIZE = 128
QUERY_GROUP = 8
SLOT = 1664
NIMG = 2
CHUNK = 512
HEADS_AT_ONCE = 4
BIG = 2.0**98


def attention_kernel(slots, piece, arrays, resumed, last, info, q_ref, flag_ref, gate_ref, *refs):
    o_ref, keys, vals, *buffers = refs[-5:]
    state_ref = refs[arrays] if resumed else None
    rows = slots * piece

    @pl.when(pl.program_id(0) == 0)
    def _():
        lane = lax.broadcasted_iota(jnp.int32, (piece, HEAD_SIZE), 1)
        row = lax.broadcasted_iota(jnp.int32, (piece, HEAD_SIZE), 0)
        ones = jnp.ones((piece, HEAD_SIZE), jnp.bfloat16)
        for j, kv in enumerate(pieces_of(refs[:arrays], piece)):
            at = slice(j * piece, (j + 1) * piece)
            position = row + info[NIMG + j] * piece
            flags = jnp.zeros((piece, HEAD_SIZE), jnp.float32)
            for i in range(NIMG):
                mine = (position >= i * SLOT) & (position < (i + 1) * SLOT)
                beyond = mine & (position - i * SLOT >= info[i])
                hit = (mine & (lane == i)) | (beyond & (lane == NIMG))
                flags = jnp.where(hit, -BIG, flags)
            keys[at, :HEAD_SIZE] = kv[:, :HEAD_SIZE]
            keys[at, HEAD_SIZE:] = flags.astype(jnp.bfloat16)
            vals[at, :HEAD_SIZE] = kv[:, HEAD_SIZE:]
            vals[at, HEAD_SIZE:] = ones

    def columns_of(g, first, count):
        at = (3 * (pl.program_id(0) * HEADS_AT_ONCE + g) + first) * HEAD_SIZE
        return pl.ds(pl.multiple_of(at, HEAD_SIZE), count * HEAD_SIZE)

    def across(tile, chunk):
        return jnp.concatenate([tile] * ((chunk.stop - chunk.start) // HEAD_SIZE), axis=1)

    scale = math.log2(math.e) / math.sqrt(HEAD_SIZE)
    gain = jnp.tanh(gate_ref[...])
    rows_q = q_ref.shape[0]
    pairs = HEADS_AT_ONCE // 2
    top = None
    for i in range(pairs + 1):
        now, later = buffers[(i + 1) % 2], buffers[i % 2]
        highest = total = None
        if i < pairs:
            wide = jnp.concatenate(
                [
                    jnp.concatenate(
                        [q_ref[:, g * HEAD_SIZE : (g + 1) * HEAD_SIZE], flag_ref[...]], axis=1
                    )
                    for g in (2 * i, 2 * i + 1)
                ],
                axis=0,
            )
        for start in range(0, rows, CHUNK):
            chunk = slice(start, min(start + CHUNK, rows))
            if i < pairs:
                part = lax.dot_general(
                    wide,
                    keys[chunk, :],
                    (((1,), (1,)), ((), ())),
                    preferred_element_type=jnp.float32,
                )
                later[:, chunk] = part
                for lane in range(0, part.shape[1], HEAD_SIZE):
                    best = part[:, lane : lane + HEAD_SIZE]
                    highest = best if highest is None else jnp.maximum(highest, best)
            if i > 0:
                weights = jnp.exp2((now[:, chunk] - across(top, chunk)) * scale).astype(jnp.bfloat16)
                term = jnp.dot(weights, vals[chunk, :], preferred_element_type=jnp.float32)
                total = term if total is None else total + term
        if i > 0:
            for half in range(2):
                g = 2 * (i - 1) + half
                mine = slice(half * rows_q, (half + 1) * rows_q)
                whole, peak = total[mine], top[mine]
                if resumed:
                    before = state_ref[:, columns_of(g, 0, 2)]
                    fade = jnp.exp2((before_top[half] - peak) * scale)
                    whole = whole + before * jnp.concatenate([fade, fade], axis=1)
                if last:
                    at = slice(g * HEAD_SIZE, (g + 1) * HEAD_SIZE)
                    out = gain * (whole[:, :HEAD_SIZE] / whole[:, HEAD_SIZE:])
                    o_ref[:, at] = out.astype(o_ref.dtype)
                else:
                    o_ref[:, columns_of(g, 0, 2)] = whole
                    o_ref[:, columns_of(g, 2, 1)] = peak
        if i < pairs:
            top = jnp.broadcast_to(jnp.max(highest, axis=1, keepdims=True), highest.shape)
            if resumed:
                before_top = [state_ref[:, columns_of(g, 2, 1)] for g in (2 * i, 2 * i + 1)]
                top = jnp.maximum(top, jnp.concatenate(before_top, axis=0))


def attend(queries, flags, gate_row, pieces, info, head, previous, state=None, last=True):
    text_rows, width = queries.shape
    piece = pieces[0].shape[0]
    rows = sum(held.shape[0] for held in pieces)
    slots = rows // piece
    steps = QUERY_GROUP // HEADS_AT_ONCE
    block = HEADS_AT_ONCE * HEAD_SIZE
    state_spec = in_vmem(1)[0]
    if last:
        out_spec = pl.BlockSpec((text_rows, block), lambda g, s: (0, head * steps + g))
        out_shape = jax.ShapeDtypeStruct((text_rows, width), jnp.bfloat16)
    else:
        out_spec = state_spec
        out_shape = jax.ShapeDtypeStruct((text_rows, 3 * QUERY_GROUP * HEAD_SIZE), jnp.float32)
    in_specs = [
        pl.BlockSpec((text_rows, block), lambda g, s: (0, head * steps + g)),
        pl.BlockSpec((text_rows, HEAD_SIZE), lambda g, s: (0, 0)),
        pl.BlockSpec((1, HEAD_SIZE), lambda g, s: (0, 0)),
    ] + in_vmem(len(pieces))
    args = [info, queries, flags, gate_row, *pieces]
    if state is not None:
        in_specs.append(state_spec)
        args.append(state)
    aliases = {}
    if previous is not None:
        in_specs.append(pl.BlockSpec(memory_space=pl.ANY))
        aliases = {len(args): 0}
        args.append(previous)
    return pl.pallas_call(
        functools.partial(
            attention_kernel, slots, piece, len(pieces), state is not None, last
        ),
        out_shape=out_shape,
        grid_spec=pltpu.PrefetchScalarGridSpec(
            num_scalar_prefetch=1,
            grid=(steps,),
            in_specs=in_specs,
            out_specs=out_spec,
            scratch_shapes=[
                pltpu.VMEM((rows, 2 * HEAD_SIZE), jnp.bfloat16),
                pltpu.VMEM((rows, 2 * HEAD_SIZE), jnp.bfloat16),
                pltpu.VMEM((2 * text_rows, rows), jnp.float32),
                pltpu.VMEM((2 * text_rows, rows), jnp.float32),
            ],
        ),
        input_output_aliases=aliases,
        compiler_params=pltpu.CompilerParams(vmem_limit_bytes=28 * 2**20),
        cost_estimate=pl.CostEstimate(
            flops=8 * QUERY_GROUP * text_rows * rows * HEAD_SIZE,
            bytes_accessed=2 * rows * 2 * HEAD_SIZE,
            transcendentals=QUERY_GROUP * text_rows * rows,
        ),
    )(*args)


def text_flags(image_lo, image_hi):
    lane = jnp.arange(HEAD_SIZE)[None, :]
    hidden = (lane < NIMG) & ((lane < image_lo[:, None]) | (lane >= image_hi[:, None]))
    return (hidden | (lane == NIMG)).astype(jnp.bfloat16)


def pick_blocks(which, image, width):
    rows = image.shape[0]
    count = which.shape[0]

    def kernel(which_ref, image_ref, o_ref, sems):
        copies = []
        for j in range(count):
            column = pl.multiple_of(which_ref[j] * width, width)
            copies.append(
                pltpu.make_async_copy(image_ref.at[:, pl.ds(column, width)], o_ref.at[j], sems.at[j])
            )
        for copy in copies:
            copy.start()
        for copy in copies:
            copy.wait()

    return pl.pallas_call(
        kernel,
        out_shape=jax.ShapeDtypeStruct((count, rows, width), image.dtype),
        grid_spec=pltpu.PrefetchScalarGridSpec(
            num_scalar_prefetch=1,
            grid=(),
            in_specs=[pl.BlockSpec(memory_space=pl.ANY)],
            out_specs=pl.BlockSpec(memory_space=pltpu.VMEM),
            scratch_shapes=[pltpu.SemaphoreType.DMA((count,))],
        ),
        compiler_params=pltpu.CompilerParams(vmem_limit_bytes=8 * 2**20),
        cost_estimate=pl.CostEstimate(
            flops=0, bytes_accessed=4 * count * rows * width, transcendentals=0
        ),
    )(which, image)


def in_vmem(count):
    return [pl.BlockSpec(memory_space=pltpu.VMEM)] * count


def pieces_of(refs, rows):
    return [ref[i : i + rows, :] for ref in refs for i in range(0, ref.shape[0], rows)]


def dots(blocks, weights):
    total = None
    for block, weight in zip(blocks, weights):
        term = jnp.dot(block, weight, preferred_element_type=jnp.float32)
        total = term if total is None else total + term
    return total


def project(core, mine, direct, passed, weights, order):
    count, rows, width = mine.shape
    columns = weights[0].shape[1]
    arrays = len(weights)

    def kernel(core_ref, mine_ref, direct_ref, passed_ref, *refs):
        other_ref, own_ref = refs[-2:]
        given = pieces_of(refs[:arrays], width)
        held = [given[order.index(j)] for j in range(count)]

        def run(*halves):
            blocks = [half[j] for half in halves for j in range(count // 2)]
            other_ref[...] = dots(blocks, held)

        @pl.when(core_ref[0] == 0)
        def _():
            run(direct_ref, passed_ref)

        @pl.when(core_ref[0] != 0)
        def _():
            run(passed_ref, direct_ref)

        own_ref[...] = dots([mine_ref[j] for j in range(count)], held)

    shape = jax.ShapeDtypeStruct((rows, columns), jnp.float32)
    return pl.pallas_call(
        kernel,
        out_shape=(shape, shape),
        in_specs=[pl.BlockSpec(memory_space=pltpu.SMEM)] + in_vmem(3 + arrays),
        out_specs=tuple(in_vmem(2)),
        compiler_params=pltpu.CompilerParams(vmem_limit_bytes=16 * 2**20),
        cost_estimate=pl.CostEstimate(
            flops=4 * count * rows * width * columns,
            bytes_accessed=4 * count * width * (rows + columns),
            transcendentals=0,
        ),
    )(core, mine, direct, passed, *weights)


def after(value, *others):
    return lax.optimization_barrier((value, *others))[0]


def swap(value, size):
    return lax.ppermute(value, "seq", [(i, i ^ 1) for i in range(size)])


def shift(value, far, near, step):
    pairs = [(f * near + n, ((f + step) % far) * near + n) for f in range(far) for n in range(near)]
    return lax.ppermute(value, "seq", pairs)


def finish(total, k_gain):
    key_head = total[:, :HEAD_SIZE]
    inverse = lax.rsqrt(jnp.mean(key_head * key_head, axis=-1, keepdims=True) + 1e-05)
    key_head = (key_head * inverse * k_gain).astype(jnp.bfloat16)
    return jnp.concatenate([key_head, total[:, HEAD_SIZE:].astype(jnp.bfloat16)], axis=1)


def per_device(
    seq_size,
    queries,
    image_token_rows,
    key_matrix,
    value_matrix,
    k_gain,
    image_counts,
    image_lo,
    image_hi,
    gate,
):
    img_rows, model_width = image_token_rows.shape
    local_heads = key_matrix.shape[1] // HEAD_SIZE
    flags = text_flags(image_lo, image_hi)
    gate_row = jnp.broadcast_to(gate[:, None], (1, HEAD_SIZE))
    group = lax.axis_index("group")
    core = lax.axis_index("head")
    index = lax.axis_index("seq")

    def head_weights(head):
        at = slice(head * HEAD_SIZE, (head + 1) * HEAD_SIZE)
        return jnp.concatenate([key_matrix[:, at], value_matrix[:, at]], axis=1)

    out = None
    if (seq_size, local_heads) != (8, 2) or img_rows % 32 or lax.axis_size("group") != 2:
        info = jnp.concatenate([image_counts, jnp.zeros((1,), jnp.int32)])
        for head in range(local_heads):
            weights = lax.all_gather(head_weights(head), "seq", axis=0, tiled=True)
            total = jnp.dot(image_token_rows, weights, preferred_element_type=jnp.float32)
            kv = lax.all_gather(finish(total, k_gain), "seq", axis=0, tiled=True)
            out = attend(queries, flags, gate_row, [kv], info, head, out)
        return out

    near = 2
    far = seq_size // near
    mine_far, mine_near = index // near, index % near
    shards = jnp.stack(
        [((mine_far - k) % far) * near + (mine_near ^ b) for k in range(far) for b in range(near)]
    ).astype(jnp.int32)
    width = model_width // seq_size // 2
    across = [(0, 1), (1, 0)]
    half = lax.dynamic_slice_in_dim(shards, core * (seq_size // 2), seq_size // 2)
    block = pick_blocks(2 * half + (1 - group), image_token_rows, width)
    direct = lax.ppermute(block, "group", across)
    parts = [
        lax.dynamic_slice_in_dim(head_weights(head), group * width, width)
        for head in range(local_heads)
    ]
    size = seq_size
    w0, w1 = parts
    a1, a3 = shift(w0, far, near, 1), shift(w0, far, near, 3)
    a0x, b0x = swap(w0, size), swap(w1, size)
    a2 = shift(after(a1, a3), far, near, 1)
    a1x = swap(after(a1, a3), size)
    a3x = swap(after(a3, a0x, b0x), size)
    b1 = shift(after(w1, a3, a0x, b0x), far, near, 1)
    mine = pick_blocks(
        after(2 * shards + group, a1, a3, a0x, b0x), image_token_rows, width
    )
    a2x = swap(after(a2, mine), size)
    b3 = shift(after(w1, a1x), far, near, 3)
    b2 = shift(b1, far, near, 1)
    b1x = shift(after(b0x, a3x), far, near, 1)
    b3x = swap(b3, size)
    passed = lax.ppermute(after(direct, a1x, a3x, a2x, b1, b3), "head", across)
    b2x = swap(b2, size)
    spreads = [[w0, a0x, a1, a1x, a2, a2x, a3, a3x], [w1, b0x, b1, b1x, b2, b2x, b3, b3x]]
    core_arg = core.reshape(1).astype(jnp.int32)
    other0, own0 = project(
        core_arg, mine, direct, passed, spreads[0], tuple(range(seq_size))
    )
    k0 = finish(own0 + lax.ppermute(other0, "group", across), k_gain)
    other1, own1 = project(
        core_arg, mine, direct, passed, after(spreads[1], k0), tuple(range(seq_size))
    )
    a1, a3, a0x = shift(k0, far, near, 1), shift(k0, far, near, 3), swap(k0, size)
    k1 = finish(own1 + after(lax.ppermute(other1, "group", across), a0x), k_gain)

    def part(head, slots, pieces, previous=None, state=None, last=True):
        here = jnp.concatenate([image_counts, jnp.stack([shards[j] for j in slots])])
        return attend(queries, flags, gate_row, pieces, here, head, previous, state, last)

    a2 = shift(a1, far, near, 1)
    ax = swap(jnp.concatenate([a1, a3]), size)
    b0x = swap(k1, size)
    b1 = shift(k1, far, near, 1)
    b3 = shift(k1, far, near, 3)
    state = part(0, (0, 1, 2, 6), [k0, a0x, a1, a3], last=False)
    a2x = swap(after(a2, state), size)
    bx = shift(jnp.concatenate([b0x, b1]), far, near, 1)
    b3x = swap(b3, size)
    b2x = swap(bx[img_rows:], size)
    out = part(0, (4, 5, 3, 7), [a2, a2x, ax], state=state)
    state = part(1, (0, 1, 2, 6), [k1, b0x, b1, b3], last=False)
    return part(1, (5, 3, 4, 7), [b2x, bx, b3x], out, state)


def solution(mesh):
    in_specs = (
        P(("group", "seq"), "head"),
        P(("group", "seq"), None),
        P("seq", "head"),
        P("seq", "head"),
        P(),
        P("group"),
        P(("group", "seq")),
        P(("group", "seq")),
        P(),
    )
    out_specs = P(("group", "seq"), "head")
    return jax.shard_map(
        functools.partial(per_device, mesh.shape["seq"]),
        mesh=mesh,
        in_specs=in_specs,
        out_specs=out_specs,
        check_vma=False,
    )
```
